512 devices in a mesh: cell: 64 (over z, y_hi, core), band: 8 (over x, y_lo).
Axes of the slice: x: 4, y: 4 (y_hi: 2, y_lo: 2; y = y_hi * 2 + y_lo), z: 16, core: 2. Of those that a mesh axis runs over, the one named last changes fastest.
Arguments:
- positions: bfloat16 [128, 3, 96, 192], P('cell', None, 'band'), may hold values from -6 to 6
- densities: bfloat16 [128, 3, 96, 192], P('cell', None, 'band'), may hold values from -6 to 6
- operator: bfloat16 [640, 96, 192], P('cell', 'band'), may hold values from -0.046875 to 0.046875
- target_shift: int32 [128, 16], P('cell'), may hold values from 0 to 191
- weights: float32 [640], replicated, may hold values from 0.02 to 0.2
Outputs:
- velocity: float32 [128, 3, 16], P('cell')
The draws below stay inside these ranges and needn't reach their ends.
All inputs are finite; a program needn't handle non-finite values.
Results may differ from the reference program's by a relative error of at most 0.0003.
Values may be sent and summed in bfloat16 or wider, within the bound.
No kernel may reach another device: no remote copies, remote signals or barrier semaphores. Data moves between devices by JAX's collectives and lax.ppermute only.
A program may use at most 64 MiB of HBM per device.

```python
import math
import jax
import jax.numpy as jnp
from jax import lax

LAT = 96
LON = 192
ROT = 640
TGT = 16
CAPS = 128


def set_ends(values, own_key, smallest, largest):
    spot = [jax.random.randint(jax.random.fold_in(own_key, axis), (), 0, length) for axis, length in enumerate(values.shape)]
    longest = values.shape.index(max(values.shape))
    neighbour = spot[:longest] + [(spot[longest] + 1) % values.shape[longest]] + spot[longest + 1:]
    return values.at[tuple(spot)].set(smallest).at[tuple(neighbour)].set(largest)


def shard_levels(own_key, shape, split, low, top_value):
    level, own = 1.0, jax.random.fold_in(own_key, 6)
    for position, shards_of in split:
        draws = jnp.exp(jax.random.uniform(jax.random.fold_in(own, position), (shards_of,), jnp.float32, low / len(split), top_value / len(split)))
        level = level * jnp.repeat(draws, shape[position] // shards_of).reshape([-1 if axis == position else 1 for axis in range(len(shape))])
    return level


def bell_draw(rng, extent, scale, most, shards=(), held_as=jnp.bfloat16):
    array = scale * jax.random.normal(rng, extent, jnp.float32)
    if shards:
        array = array * shard_levels(rng, extent, shards, -0.22, 0.18)
    return jnp.clip(array, -most, most).astype(held_as)


def setup_inputs(seed: int = 0) -> dict:
    seeds = jax.random.split(jax.random.key(seed), 6)
    positions = bell_draw(seeds[0], (CAPS, 3, LAT, LON), 1.0, 6.0, ((0, 64), (2, 8)))
    densities = bell_draw(seeds[1], (CAPS, 3, LAT, LON), 1.0, 6.0, ((0, 64), (2, 8)))
    operator = bell_draw(seeds[2], (ROT, LAT, LON), (LAT * LON) ** -0.5, 0.046875, ((0, 64), (1, 8)))
    target_shift = set_ends(jax.random.randint(seeds[3], (CAPS, TGT), 0, LON), jax.random.fold_in(seeds[3], 1), 0, LON - 1).astype(jnp.int32)
    weights = jnp.clip(jnp.exp(jax.random.uniform(seeds[4], (ROT,), jnp.float32, math.log(0.02), math.log(0.2))), 0.02, 0.2)
    return dict(positions=positions, densities=densities, operator=operator, target_shift=target_shift, weights=weights)


blob_radius = 0.5


def stokes(target, rows, weights):
    spread = target[:, :, :, None] - rows[:, 0:3]
    force = rows[:, 3:6]
    dist_sq = jnp.sum(spread * spread, axis=1)
    along = jnp.sum(spread * force, axis=1)
    blob_sq = blob_radius * blob_radius
    numer = (dist_sq + 2.0 * blob_sq)[:, None] * force + along[:, None] * spread
    kernel = weights / (dist_sq + blob_sq) ** 1.5
    return jnp.sum(numer * kernel[:, None], axis=-1)


def reference(positions, densities, operator, target_shift, weights):
    op_rows = operator.reshape(ROT, LAT * LON)

    def one_capsule(triple):
        posit, dense, shifts = triple
        source = jnp.concatenate([posit, dense], axis=0)
        indices = (jnp.arange(LON, dtype=jnp.int32)[None, :] + shifts[:, None]) % LON
        rolled = jnp.take(source, indices, axis=2)
        rolled = jnp.transpose(rolled, (0, 2, 1, 3)).reshape(6 * TGT, LAT * LON)
        result = lax.dot_general(rolled, op_rows, (((1,), (1,)), ((), ())), preferred_element_type=jnp.float32)
        return result.reshape(6, TGT, ROT)

    rotated = lax.map(one_capsule, (positions, densities, target_shift))
    return stokes(rotated[:, 0:3, :, 0], rotated, weights)
```

```python
import jax
import jax.numpy as jnp
from jax import lax
from jax.experimental import pallas as pl
from jax.experimental.pallas import tpu as pltpu
from jax.sharding import Mesh
from jax.sharding import PartitionSpec as P

F32 = jnp.float32
BF16 = jnp.bfloat16

LAT_HERE = 12
LON = 192
COLS = LAT_HERE * LON
TGT = 16
ROWS_HERE = 10
SLOT = 16
Z = 16
QUAD = 4
BAND = 8
CAPS = 2 * QUAD
NODES = Z * ROWS_HERE

CELL = ("z", "y_hi", "core")
GROUP = ("y_hi", "core")
STRIP = ("x", "y_lo")

blob_radius = 0.5


def rotate_kernel(src_ref, shift_ref, op_ref, out_ref, tiles, rolled, acc):
    for p in range(QUAD):
        block = src_ref[p].astype(F32)
        here = pl.ds(p * 144, 144)
        tiles[0, here, :] = block[:, 0:128]
        tiles[1, here, :] = jnp.concatenate([block[:, 128:192], block[:, 0:64]], axis=1)
        tiles[2, here, :] = block[:, 64:192]

    lane = lax.broadcasted_iota(jnp.int32, (TGT, 128), 1)
    low_half = lane < 64

    def per_capsule(c, carry):
        shift = jnp.broadcast_to(shift_ref[pl.ds(pl.multiple_of(c * TGT, TGT), TGT), :], (TGT, 128))
        place = lane + shift
        even = jnp.bitwise_and(place, 127)
        odd = jnp.bitwise_and(place + 64, 127)
        e0, e1, e2 = place < 128, place < 256, place + 128 < 256
        h0, h1 = place - 64 < 128, place + 64 < 256
        h2 = place + 64 < 128

        def per_component(k, carry):
            base = c * 72 + k * LAT_HERE
            to = pl.ds(pl.multiple_of((c * 6 + k) * TGT, TGT), TGT)
            for m in range(LAT_HERE // 2):

                def picked(a, where):
                    return [
                        jnp.take_along_axis(
                            jnp.broadcast_to(tiles[q, pl.ds(base + a, 1), :], (TGT, 128)),
                            where,
                            axis=1,
                            mode="promise_in_bounds",
                        )
                        for q in range(3)
                    ]

                g = picked(2 * m, even)
                h = picked(2 * m + 1, odd)
                first = jnp.where(e0, g[0], jnp.where(e1, g[1], g[2]))
                middle = jnp.where(low_half, jnp.where(e2, g[1], g[2]), jnp.where(h0, h[0], h[1]))
                last = jnp.where(h2, h[0], jnp.where(h1, h[1], h[2]))
                for n, value in enumerate((first, middle, last)):
                    rolled[to, pl.ds((3 * m + n) * 128, 128)] = value.astype(BF16)
            return carry

        return lax.fori_loop(0, 6, per_component, carry)

    lax.fori_loop(0, CAPS, per_capsule, 0)

    slot = lax.broadcasted_iota(jnp.int32, (NODES, Z * SLOT), 1)
    node = lax.broadcasted_iota(jnp.int32, (NODES, Z * SLOT), 0)
    within = jnp.bitwise_and(slot, SLOT - 1)
    kept = jnp.right_shift(slot, 4) * ROWS_HERE + within
    chosen = jnp.where((kept == node) & (within < ROWS_HERE), 1.0, 0.0).astype(BF16)
    held = jnp.dot(chosen, op_ref[...], preferred_element_type=F32).astype(BF16)
    acc[...] = lax.dot_general(
        rolled[...], held, (((1,), (1,)), ((), ())), preferred_element_type=F32
    )

    upper = lax.broadcasted_iota(jnp.int32, (8, NODES), 0) < 4
    for c in range(CAPS):
        for half in range(2):
            tails = [[], []]
            for pair in range(3):
                at = c * 96 + pair * 32 + half * 8
                one = acc[at : at + 8, :]
                two = acc[at + 16 : at + 24, :]
                lo = jnp.where(upper, one, pltpu.roll(two, 4, 0))
                hi = jnp.where(upper, pltpu.roll(one, 4, 0), two)
                for j, tile in enumerate((lo, hi)):
                    dest = (c // 2) * BAND + (c % 2) * 4 + half * 2 + j
                    out_ref[dest, pair * 8 : pair * 8 + 8, :] = tile[:, 0:128]
                    tails[j].append(tile[:, 128:NODES])
            for j in range(2):
                dest = (c // 2) * BAND + (c % 2) * 4 + half * 2 + j
                blank = jnp.zeros((8, 32), F32)
                out_ref[dest, 24:32, :] = jnp.concatenate([*tails[j], blank], axis=1)


def stokes_kernel(parts_ref, weight_ref, out_ref):
    blob_sq = blob_radius * blob_radius
    total = jnp.zeros((3, 4, 1), F32)
    pole = None
    sums = [jnp.zeros((4, 1), F32) for _ in range(3)]
    for g in range(QUAD):
        whole = parts_ref[g, 0]
        for b in range(1, BAND):
            whole = whole + parts_ref[g, b]
        main = [whole[4 * k : 4 * k + 4, :] for k in range(6)]
        tail = whole[24:32, :]
        rest = [
            tail[4 * (k % 2) : 4 * (k % 2) + 4, 32 * (k // 2) : 32 * (k // 2) + 32] for k in range(6)
        ]
        if g == 0:
            pole = [main[k][:, 0:1] for k in range(3)]
        for rows, weights in (
            (main, weight_ref[g : g + 1, 0:128]),
            (rest, weight_ref[g : g + 1, 128:NODES]),
        ):
            d = [pole[k] - rows[k] for k in range(3)]
            f = rows[3:6]
            q = d[0] * d[0] + d[1] * d[1] + d[2] * d[2]
            along = d[0] * f[0] + d[1] * f[1] + d[2] * f[2]
            s = q + blob_sq
            r = lax.rsqrt(s)
            kernel = weights * (r * r * r)
            near = (q + 2.0 * blob_sq) * kernel
            along = along * kernel
            for k in range(3):
                sums[k] = sums[k] + jnp.sum(near * f[k] + along * d[k], axis=1, keepdims=True)
    lane = lax.broadcasted_iota(jnp.int32, (4, 128), 1)
    packed = jnp.where(lane == 0, sums[0], jnp.where(lane == 1, sums[1], sums[2]))
    packed = jnp.concatenate([packed, jnp.zeros((4, 128), F32)], axis=0)
    for b in range(BAND):
        out_ref[b] = packed


def per_device(positions, densities, operator, target_shift, weights):
    vmem = pl.BlockSpec(memory_space=pltpu.VMEM)
    source = jnp.concatenate([positions, densities], axis=1).reshape(144, LON)
    source = lax.all_to_all(
        jnp.broadcast_to(source[None], (QUAD, 144, LON)), GROUP, 0, 0, tiled=True
    )
    shifts = lax.all_to_all(
        jnp.broadcast_to(target_shift[None], (QUAD, 2, TGT)), GROUP, 0, 0, tiled=True
    )
    rows = jnp.pad(operator.reshape(ROWS_HERE, COLS), ((0, SLOT - ROWS_HERE), (0, 0)))
    rows = lax.all_gather(rows, "z", axis=0, tiled=True)
    parts = pl.pallas_call(
        rotate_kernel,
        out_shape=jax.ShapeDtypeStruct((QUAD * BAND, 32, 128), F32),
        in_specs=[vmem] * 3,
        out_specs=vmem,
        scratch_shapes=[
            pltpu.VMEM((3, QUAD * 144, 128), F32),
            pltpu.VMEM((CAPS * 6 * TGT, COLS), BF16),
            pltpu.VMEM((CAPS * 6 * TGT, NODES), F32),
        ],
        compiler_params=pltpu.CompilerParams(vmem_limit_bytes=48 * 2**20),
        name="rotate",
    )(source, shifts.reshape(CAPS * TGT, 1), rows)
    parts = lax.all_to_all(parts, GROUP + STRIP, 0, 0, tiled=True)
    weights = weights.reshape(Z, QUAD, ROWS_HERE).transpose(1, 0, 2).reshape(QUAD, NODES)
    found = pl.pallas_call(
        stokes_kernel,
        out_shape=jax.ShapeDtypeStruct((BAND, 8, 128), F32),
        in_specs=[vmem] * 2,
        out_specs=vmem,
        compiler_params=pltpu.CompilerParams(vmem_limit_bytes=32 * 2**20),
        name="stokes",
    )(parts.reshape(QUAD, BAND, 32, 128), weights)
    found = lax.all_to_all(found, STRIP, 0, 0, tiled=True)
    return found[:, 0:4, 0:3].reshape(2, TGT, 3).transpose(0, 2, 1)


def solution(mesh):
    split = Mesh(mesh.devices.reshape(16, 2, 2, 4, 2), CELL + STRIP)
    in_specs = (
        P(CELL, None, STRIP, None),
        P(CELL, None, STRIP, None),
        P(CELL, STRIP, None),
        P(CELL, None),
        P(),
    )
    return jax.shard_map(
        per_device, mesh=split, in_specs=in_specs, out_specs=P(CELL, None, None), check_vma=False
    )
```

```python
import jax
import jax.numpy as jnp
from jax import lax
from jax.experimental import pallas as pl
from jax.experimental.pallas import tpu as pltpu
from jax.sharding import Mesh
from jax.sharding import PartitionSpec as P

F32 = jnp.float32
BF16 = jnp.bfloat16

LAT_HERE = 12
LON = 192
COLS = LAT_HERE * LON
TGT = 16
ROWS_HERE = 10
Z = 16
QUAD = 4
BAND = 8
CAPS = 2 * QUAD
NODES = Z * ROWS_HERE
LINES = ROWS_HERE * COLS // 128

CELL = ("z", "y_hi", "core")
GROUP = ("y_hi", "core")
STRIP = ("x", "y_lo")

blob_radius = 0.5


def roll_kernel(src_ref, rolled_ref, tiles):
    for p in range(QUAD):
        block = src_ref[p, 0:144, :].astype(F32)
        here = pl.ds(p * 144, 144)
        tiles[0, here, :] = block[:, 0:128]
        tiles[1, here, :] = jnp.concatenate([block[:, 128:192], block[:, 0:64]], axis=1)
        tiles[2, here, :] = block[:, 64:192]

    lane = lax.broadcasted_iota(jnp.int32, (TGT, 128), 1)
    low_half = lane < 64

    for c in range(CAPS):
        at = (c % 2) * 96
        shift = src_ref[c // 2, 144:160, at : at + 1].astype(F32).astype(jnp.int32)
        place = lane + jnp.broadcast_to(shift, (TGT, 128))
        even = jnp.bitwise_and(place, 127)
        odd = jnp.bitwise_and(place + 64, 127)
        e0, e1, e2 = place < 128, place < 256, place + 128 < 256
        h0, h1 = place - 64 < 128, place + 64 < 256
        h2 = place + 64 < 128

        def per_component(k, carry):
            base = c * 72 + k * LAT_HERE
            to = pl.ds(pl.multiple_of((c * 6 + k) * TGT, TGT), TGT)
            for m in range(LAT_HERE // 2):

                def picked(a, where):
                    return [
                        jnp.take_along_axis(
                            jnp.broadcast_to(tiles[q, pl.ds(base + a, 1), :], (TGT, 128)),
                            where,
                            axis=1,
                            mode="promise_in_bounds",
                        )
                        for q in range(3)
                    ]

                g = picked(2 * m, even)
                h = picked(2 * m + 1, odd)
                first = jnp.where(e0, g[0], jnp.where(e1, g[1], g[2]))
                middle = jnp.where(low_half, jnp.where(e2, g[1], g[2]), jnp.where(h0, h[0], h[1]))
                last = jnp.where(h2, h[0], jnp.where(h1, h[1], h[2]))
                for n, value in enumerate((first, middle, last)):
                    rolled_ref[to, pl.ds((3 * m + n) * 128, 128)] = value.astype(BF16)
            return carry

        lax.fori_loop(0, 6, per_component, 0)


def rotate_kernel(rolled_ref, op_ref, out_ref, lines, held, acc):
    for z in range(Z):
        lines[z * LINES : (z + 1) * LINES, :] = op_ref[z].astype(F32)
    for n in range(COLS // 128):
        rows = lines[pl.ds(n, NODES, stride=COLS // 128), :]
        held[:, n * 128 : (n + 1) * 128] = rows.astype(BF16)
    acc[...] = lax.dot_general(
        rolled_ref[...], held[...], (((1,), (1,)), ((), ())), preferred_element_type=F32
    )

    upper = lax.broadcasted_iota(jnp.int32, (8, NODES), 0) < 4
    for c in range(CAPS):
        for half in range(2):
            tails = [[], []]
            for pair in range(3):
                at = c * 96 + pair * 32 + half * 8
                one = acc[at : at + 8, :]
                two = acc[at + 16 : at + 24, :]
                lo = jnp.where(upper, one, pltpu.roll(two, 4, 0))
                hi = jnp.where(upper, pltpu.roll(one, 4, 0), two)
                for j, tile in enumerate((lo, hi)):
                    dest = (c // 2) * BAND + (c % 2) * 4 + half * 2 + j
                    out_ref[dest, pair * 8 : pair * 8 + 8, :] = tile[:, 0:128]
                    tails[j].append(tile[:, 128:NODES])
            for j in range(2):
                dest = (c // 2) * BAND + (c % 2) * 4 + half * 2 + j
                blank = jnp.zeros((8, 32), F32)
                out_ref[dest, 24:32, :] = jnp.concatenate([*tails[j], blank], axis=1)


def stokes_kernel(parts_ref, weight_ref, out_ref):
    blob_sq = blob_radius * blob_radius
    total = jnp.zeros((3, 4, 1), F32)
    pole = None
    sums = [jnp.zeros((4, 1), F32) for _ in range(3)]
    for g in range(QUAD):
        whole = parts_ref[g, 0]
        for b in range(1, BAND):
            whole = whole + parts_ref[g, b]
        main = [whole[4 * k : 4 * k + 4, :] for k in range(6)]
        tail = whole[24:32, :]
        rest = [
            tail[4 * (k % 2) : 4 * (k % 2) + 4, 32 * (k // 2) : 32 * (k // 2) + 32] for k in range(6)
        ]
        if g == 0:
            pole = [main[k][:, 0:1] for k in range(3)]
        for rows, weights in (
            (main, weight_ref[g : g + 1, 0:128]),
            (rest, weight_ref[g : g + 1, 128:NODES]),
        ):
            d = [pole[k] - rows[k] for k in range(3)]
            f = rows[3:6]
            q = d[0] * d[0] + d[1] * d[1] + d[2] * d[2]
            along = d[0] * f[0] + d[1] * f[1] + d[2] * f[2]
            s = q + blob_sq
            r = lax.rsqrt(s)
            kernel = weights * (r * r * r)
            near = (q + 2.0 * blob_sq) * kernel
            along = along * kernel
            for k in range(3):
                sums[k] = sums[k] + jnp.sum(near * f[k] + along * d[k], axis=1, keepdims=True)
    lane = lax.broadcasted_iota(jnp.int32, (4, 128), 1)
    packed = jnp.where(lane == 0, sums[0], jnp.where(lane == 1, sums[1], sums[2]))
    packed = jnp.concatenate([packed, jnp.zeros((4, 128), F32)], axis=0)
    for b in range(BAND):
        out_ref[b] = packed


def per_device(positions, densities, operator, target_shift, weights):
    vmem = pl.BlockSpec(memory_space=pltpu.VMEM)
    lines = operator.reshape(LINES, 128)
    lines = lax.all_gather(lines[None], "z", axis=0, tiled=True)
    source = jnp.concatenate([positions, densities], axis=1).reshape(144, LON)
    shifts = jnp.broadcast_to(target_shift.T[:, :, None], (TGT, 2, LON // 2)).reshape(TGT, LON)
    source = jnp.concatenate([source, shifts.astype(BF16)], axis=0)
    source = lax.all_to_all(
        jnp.broadcast_to(source[None], (QUAD, *source.shape)), GROUP, 0, 0, tiled=True
    )
    rolled = pl.pallas_call(
        roll_kernel,
        out_shape=jax.ShapeDtypeStruct((CAPS * 6 * TGT, COLS), BF16),
        in_specs=[vmem],
        out_specs=vmem,
        scratch_shapes=[pltpu.VMEM((3, QUAD * 144, 128), F32)],
        compiler_params=pltpu.CompilerParams(vmem_limit_bytes=32 * 2**20),
        cost_estimate=pl.CostEstimate(flops=10**9, bytes_accessed=2**23, transcendentals=0),
        name="roll",
    )(source)
    parts = pl.pallas_call(
        rotate_kernel,
        out_shape=jax.ShapeDtypeStruct((QUAD * BAND, 32, 128), F32),
        in_specs=[vmem] * 2,
        out_specs=vmem,
        scratch_shapes=[
            pltpu.VMEM((Z * LINES, 128), F32),
            pltpu.VMEM((NODES, COLS), BF16),
            pltpu.VMEM((CAPS * 6 * TGT, NODES), F32),
        ],
        compiler_params=pltpu.CompilerParams(vmem_limit_bytes=32 * 2**20),
        name="rotate",
    )(rolled, lines)
    parts = lax.all_to_all(parts, GROUP + STRIP, 0, 0, tiled=True)
    weights = weights.reshape(Z, QUAD, ROWS_HERE).transpose(1, 0, 2).reshape(QUAD, NODES)
    found = pl.pallas_call(
        stokes_kernel,
        out_shape=jax.ShapeDtypeStruct((BAND, 8, 128), F32),
        in_specs=[vmem] * 2,
        out_specs=vmem,
        compiler_params=pltpu.CompilerParams(vmem_limit_bytes=32 * 2**20),
        name="stokes",
    )(parts.reshape(QUAD, BAND, 32, 128), weights)
    found = lax.all_to_all(found, STRIP, 0, 0, tiled=True)
    return found[:, 0:4, 0:3].reshape(2, TGT, 3).transpose(0, 2, 1)


def solution(mesh):
    split = Mesh(mesh.devices.reshape(16, 2, 2, 4, 2), CELL + STRIP)
    in_specs = (
        P(CELL, None, STRIP, None),
        P(CELL, None, STRIP, None),
        P(CELL, STRIP, None),
        P(CELL, None),
        P(),
    )
    return jax.shard_map(
        per_device, mesh=split, in_specs=in_specs, out_specs=P(CELL, None, None), check_vma=False
    )
```

```python
import jax
import jax.numpy as jnp
from jax import lax
from jax.experimental import pallas as pl
from jax.experimental.pallas import tpu as pltpu
from jax.sharding import Mesh
from jax.sharding import PartitionSpec as P

F32 = jnp.float32
BF16 = jnp.bfloat16

LAT_HERE = 12
LON = 192
COLS = LAT_HERE * LON
TGT = 16
ROWS_HERE = 10
Z = 16
QUAD = 4
BAND = 8
CAPS = 2 * QUAD
NODES = Z * ROWS_HERE
LINES = ROWS_HERE * COLS // 128

CELL = ("z", "y_hi", "core")
GROUP = ("y_hi", "core")
STRIP = ("x", "y_lo")

blob_radius = 0.5


def roll_kernel(src_ref, rolled_ref, tiles):
    for p in range(QUAD):
        block = src_ref[p, 0:144, :].astype(F32)
        here = pl.ds(p * 144, 144)
        tiles[0, here, :] = block[:, 0:128]
        tiles[1, here, :] = jnp.concatenate([block[:, 128:192], block[:, 0:64]], axis=1)
        tiles[2, here, :] = block[:, 64:192]

    lane = lax.broadcasted_iota(jnp.int32, (TGT, 128), 1)
    low_half = lane < 64

    for c in range(CAPS):
        at = (c % 2) * 96
        shift = src_ref[c // 2, 144:160, at : at + 1].astype(F32).astype(jnp.int32)
        place = lane + jnp.broadcast_to(shift, (TGT, 128))
        even = jnp.bitwise_and(place, 127)
        odd = jnp.bitwise_and(place + 64, 127)
        e0, e1, e2 = place < 128, place < 256, place + 128 < 256
        h0, h1 = place - 64 < 128, place + 64 < 256
        h2 = place + 64 < 128

        def per_component(k, carry):
            base = c * 72 + k * LAT_HERE
            to = pl.ds(pl.multiple_of((c * 6 + k) * TGT, TGT), TGT)
            for m in range(LAT_HERE // 2):

                def picked(a, where):
                    return [
                        jnp.take_along_axis(
                            jnp.broadcast_to(tiles[q, pl.ds(base + a, 1), :], (TGT, 128)),
                            where,
                            axis=1,
                            mode="promise_in_bounds",
                        )
                        for q in range(3)
                    ]

                g = picked(2 * m, even)
                h = picked(2 * m + 1, odd)
                first = jnp.where(e0, g[0], jnp.where(e1, g[1], g[2]))
                middle = jnp.where(low_half, jnp.where(e2, g[1], g[2]), jnp.where(h0, h[0], h[1]))
                last = jnp.where(h2, h[0], jnp.where(h1, h[1], h[2]))
                for n, value in enumerate((first, middle, last)):
                    rolled_ref[to, pl.ds((3 * m + n) * 128, 128)] = value.astype(BF16)
            return carry

        lax.fori_loop(0, 6, per_component, 0)


def rotate_kernel(rolled_ref, op_ref, weight_ref, out_ref, weight_out_ref, lines, held, acc):
    weight_out_ref[...] = weight_ref[...]
    for z in range(Z):
        lines[z * LINES : (z + 1) * LINES, :] = op_ref[z].astype(F32)
    for n in range(COLS // 128):
        rows = lines[pl.ds(n, NODES, stride=COLS // 128), :]
        held[:, n * 128 : (n + 1) * 128] = rows.astype(BF16)
    acc[...] = lax.dot_general(
        rolled_ref[...], held[...], (((1,), (1,)), ((), ())), preferred_element_type=F32
    )

    upper = lax.broadcasted_iota(jnp.int32, (8, NODES), 0) < 4
    for c in range(CAPS):
        for half in range(2):
            tails = [[], []]
            for pair in range(3):
                at = c * 96 + pair * 32 + half * 8
                one = acc[at : at + 8, :]
                two = acc[at + 16 : at + 24, :]
                lo = jnp.where(upper, one, pltpu.roll(two, 4, 0))
                hi = jnp.where(upper, pltpu.roll(one, 4, 0), two)
                for j, tile in enumerate((lo, hi)):
                    dest = (c // 2) * BAND + (c % 2) * 4 + half * 2 + j
                    out_ref[dest, pair * 8 : pair * 8 + 8, :] = tile[:, 0:128]
                    tails[j].append(tile[:, 128:NODES])
            for j in range(2):
                dest = (c // 2) * BAND + (c % 2) * 4 + half * 2 + j
                blank = jnp.zeros((8, 32), F32)
                out_ref[dest, 24:32, :] = jnp.concatenate([*tails[j], blank], axis=1)


def stokes_kernel(parts_ref, weight_ref, out_ref):
    blob_sq = blob_radius * blob_radius
    total = jnp.zeros((3, 4, 1), F32)
    pole = None
    sums = [jnp.zeros((4, 1), F32) for _ in range(3)]
    for g in range(QUAD):
        whole = parts_ref[g, 0]
        for b in range(1, BAND):
            whole = whole + parts_ref[g, b]
        main = [whole[4 * k : 4 * k + 4, :] for k in range(6)]
        tail = whole[24:32, :]
        rest = [
            tail[4 * (k % 2) : 4 * (k % 2) + 4, 32 * (k // 2) : 32 * (k // 2) + 32] for k in range(6)
        ]
        if g == 0:
            pole = [main[k][:, 0:1] for k in range(3)]
        for rows, weights in (
            (main, weight_ref[g : g + 1, 0:128]),
            (rest, weight_ref[g : g + 1, 128:NODES]),
        ):
            d = [pole[k] - rows[k] for k in range(3)]
            f = rows[3:6]
            q = d[0] * d[0] + d[1] * d[1] + d[2] * d[2]
            along = d[0] * f[0] + d[1] * f[1] + d[2] * f[2]
            s = q + blob_sq
            r = lax.rsqrt(s)
            kernel = weights * (r * r * r)
            near = (q + 2.0 * blob_sq) * kernel
            along = along * kernel
            for k in range(3):
                sums[k] = sums[k] + jnp.sum(near * f[k] + along * d[k], axis=1, keepdims=True)
    lane = lax.broadcasted_iota(jnp.int32, (4, 128), 1)
    packed = jnp.where(lane == 0, sums[0], jnp.where(lane == 1, sums[1], sums[2]))
    packed = jnp.concatenate([packed, jnp.zeros((4, 128), F32)], axis=0)
    for b in range(BAND):
        out_ref[b] = packed


def per_device(positions, densities, operator, target_shift, weights):
    vmem = pl.BlockSpec(memory_space=pltpu.VMEM)
    lines = jnp.broadcast_to(operator.reshape(LINES, 128)[None], (Z, LINES, 128))
    lines, positions, densities, target_shift, weights = lax.optimization_barrier(
        (lines, positions, densities, target_shift, weights)
    )
    lines = lax.all_to_all(lines, "z", 0, 0, tiled=True)
    weights = weights.reshape(Z, QUAD, ROWS_HERE).transpose(1, 0, 2).reshape(QUAD, NODES)
    source = jnp.concatenate([positions, densities], axis=1).reshape(144, LON)
    shifts = jnp.broadcast_to(target_shift.T[:, :, None], (TGT, 2, LON // 2)).reshape(TGT, LON)
    source = jnp.concatenate([source, shifts.astype(BF16)], axis=0)
    source = lax.all_gather(source[None], GROUP, axis=0, tiled=True)
    rolled = pl.pallas_call(
        roll_kernel,
        out_shape=jax.ShapeDtypeStruct((CAPS * 6 * TGT, COLS), BF16),
        in_specs=[vmem],
        out_specs=vmem,
        scratch_shapes=[pltpu.VMEM((3, QUAD * 144, 128), F32)],
        compiler_params=pltpu.CompilerParams(vmem_limit_bytes=32 * 2**20),
        cost_estimate=pl.CostEstimate(flops=10**9, bytes_accessed=2**23, transcendentals=0),
        name="roll",
    )(source)
    parts, weights = pl.pallas_call(
        rotate_kernel,
        out_shape=(
            jax.ShapeDtypeStruct((QUAD * BAND, 32, 128), F32),
            jax.ShapeDtypeStruct((QUAD, NODES), F32),
        ),
        in_specs=[vmem] * 3,
        out_specs=(vmem, vmem),
        scratch_shapes=[
            pltpu.VMEM((Z * LINES, 128), F32),
            pltpu.VMEM((NODES, COLS), BF16),
            pltpu.VMEM((CAPS * 6 * TGT, NODES), F32),
        ],
        compiler_params=pltpu.CompilerParams(vmem_limit_bytes=32 * 2**20),
        name="rotate",
    )(rolled, lines, weights)
    parts = lax.all_to_all(parts, GROUP + STRIP, 0, 0, tiled=True)
    found = pl.pallas_call(
        stokes_kernel,
        out_shape=jax.ShapeDtypeStruct((BAND, 8, 128), F32),
        in_specs=[vmem] * 2,
        out_specs=vmem,
        compiler_params=pltpu.CompilerParams(vmem_limit_bytes=32 * 2**20),
        name="stokes",
    )(parts.reshape(QUAD, BAND, 32, 128), weights)
    found = lax.all_to_all(found, STRIP, 0, 0, tiled=True)
    return found[:, 0:4, 0:3].reshape(2, TGT, 3).transpose(0, 2, 1)


def solution(mesh):
    split = Mesh(mesh.devices.reshape(16, 2, 2, 4, 2), CELL + STRIP)
    in_specs = (
        P(CELL, None, STRIP, None),
        P(CELL, None, STRIP, None),
        P(CELL, STRIP, None),
        P(CELL, None),
        P(),
    )
    return jax.shard_map(
        per_device, mesh=split, in_specs=in_specs, out_specs=P(CELL, None, None), check_vma=False
    )
```

```python
import jax
import jax.numpy as jnp
from jax import lax
from jax.experimental import pallas as pl
from jax.experimental.pallas import tpu as pltpu
from jax.sharding import Mesh
from jax.sharding import PartitionSpec as P

F32 = jnp.float32
BF16 = jnp.bfloat16

LAT_HERE = 12
LON = 192
COLS = LAT_HERE * LON
TGT = 16
ROWS_HERE = 10
Z = 8
QUAD = 4
PARITY = 2
GROUPS = PARITY * QUAD
BAND = 8
HALF_CAPS = 2 * QUAD
NODES = Z * ROWS_HERE
TILES = COLS // 128
LINES = ROWS_HERE * TILES
LEFT = 128 - NODES

CELL = ("z_half", "z_low", "y_hi", "core")
GROUP = ("y_hi", "core")
STRIP = ("x", "y_lo")

blob_radius = 0.5


def pack_kernel(op_ref, out_ref, lines):
    for r in range(ROWS_HERE):
        row = op_ref[r].astype(F32)
        high = row[:, 128:LON]
        at = r * TILES
        lines[at : at + LAT_HERE, :] = row[:, 0:128]
        lines[at + LAT_HERE : at + TILES, :] = jnp.concatenate([high[0:6], high[6:12]], axis=1)
    packed = lines[...].astype(BF16)
    for z in range(Z):
        out_ref[z] = packed


def roll_kernel(src_ref, rolled_ref, tiles):
    for p in range(QUAD):
        block = src_ref[p, 0:144, :].astype(F32)
        here = pl.ds(p * 144, 144)
        tiles[0, here, :] = block[:, 0:128]
        tiles[1, here, :] = jnp.concatenate([block[:, 128:192], block[:, 0:64]], axis=1)
        tiles[2, here, :] = block[:, 64:192]

    lane = lax.broadcasted_iota(jnp.int32, (TGT, 128), 1)

    for c in range(HALF_CAPS):
        column = (c % 2) * 96
        shift = src_ref[c // 2, 144:160, column : column + 1].astype(F32).astype(jnp.int32)
        shift = jnp.broadcast_to(shift, (TGT, 128))
        take = jnp.bitwise_and(lane + shift, 127)
        goal = jnp.bitwise_and(lane - shift, 127)
        place = goal + shift
        early, late, low = place < 128, place < 256, goal < 64

        def rolled(value):
            return jnp.take_along_axis(value, take, axis=1, mode="promise_in_bounds").astype(BF16)

        def per_component(k, carry):
            base = c * 72 + k * LAT_HERE
            to = pl.ds(pl.multiple_of((c * 6 + k) * TGT, TGT), TGT)

            def row(q, a):
                return jnp.broadcast_to(tiles[q, pl.ds(base + a, 1), :], (TGT, 128))

            for m in range(6):
                t = [row(q, m) for q in range(3)]
                u = [row(q, m + 6) for q in range(3)]
                first = jnp.where(early, t[0], jnp.where(late, t[1], t[2]))
                second = jnp.where(early, u[0], jnp.where(late, u[1], u[2]))
                high = jnp.where(
                    low,
                    jnp.where(early, t[1], t[2]),
                    jnp.where(early, u[2], jnp.where(late, u[0], u[1])),
                )
                rolled_ref[to, m * 128 : m * 128 + 128] = rolled(first)
                rolled_ref[to, (m + 6) * 128 : (m + 6) * 128 + 128] = rolled(second)
                rolled_ref[to, (m + 12) * 128 : (m + 12) * 128 + 128] = rolled(high)
            return carry

        lax.fori_loop(0, 6, per_component, 0)


def rotate_kernel(
    mine_ref, next_ref, op_ref, weight_ref, side_ref, out_ref, weight_out_ref, lines, held, acc
):
    weight_out_ref[...] = weight_ref[...]
    for z in range(Z):
        lines[z * LINES : (z + 1) * LINES, :] = op_ref[z].astype(F32)
    for n in range(TILES):
        held[:, n * 128 : (n + 1) * 128] = lines[pl.ds(n, NODES, stride=TILES), :].astype(BF16)
    side = side_ref[0]
    upper = lax.broadcasted_iota(jnp.int32, (8, NODES), 0) < 4
    blank = jnp.zeros((8, 2 * 128 - 3 * NODES), F32)
    for o, rolled_ref in enumerate((mine_ref, next_ref)):
        acc[o] = lax.dot_general(
            rolled_ref[...], held[...], (((1,), (1,)), ((), ())), preferred_element_type=F32
        )
        first = jnp.bitwise_xor(side, o) * (QUAD * BAND)
        for c in range(HALF_CAPS):
            for half in range(2):
                found = [[], []]
                for pair in range(3):
                    at = c * 96 + pair * 32 + half * 8
                    one = acc[o, at : at + 8, :]
                    two = acc[o, at + 16 : at + 24, :]
                    found[0].append(jnp.where(upper, one, pltpu.roll(two, 4, 0)))
                    found[1].append(jnp.where(upper, pltpu.roll(one, 4, 0), two))
                for j in range(2):
                    dest = first + ((c // 2) * BAND + (c % 2) * 4 + half * 2 + j)
                    a, b, d = found[j]
                    out_ref[dest, 0:8, :] = jnp.concatenate([a, b[:, 0:LEFT]], axis=1)
                    out_ref[dest, 8:16, :] = jnp.concatenate([b[:, LEFT:NODES], d, blank], axis=1)


def stokes_kernel(parts_ref, weight_ref, out_ref):
    blob_sq = blob_radius * blob_radius
    pole = None
    sums = [jnp.zeros((4, 1), F32) for _ in range(3)]
    for g in range(GROUPS):
        whole = parts_ref[g, 0]
        for b in range(1, BAND):
            whole = whole + parts_ref[g, b]
        one, two = whole[0:8, :], whole[8:16, :]
        rest = NODES - LEFT
        pairs = (
            one[:, 0:NODES],
            jnp.concatenate([one[:, NODES:128], two[:, 0:rest]], axis=1),
            two[:, rest : rest + NODES],
        )
        rows = [pairs[k // 2][4 * (k % 2) : 4 * (k % 2) + 4, :] for k in range(6)]
        if g == 0:
            pole = [rows[k][:, 0:1] for k in range(3)]
        weights = weight_ref[g : g + 1, :]
        d = [pole[k] - rows[k] for k in range(3)]
        f = rows[3:6]
        q = d[0] * d[0] + d[1] * d[1] + d[2] * d[2]
        along = d[0] * f[0] + d[1] * f[1] + d[2] * f[2]
        r = lax.rsqrt(q + blob_sq)
        kernel = weights * (r * r * r)
        near = (q + 2.0 * blob_sq) * kernel
        along = along * kernel
        for k in range(3):
            sums[k] = sums[k] + jnp.sum(near * f[k] + along * d[k], axis=1, keepdims=True)
    lane = lax.broadcasted_iota(jnp.int32, (4, 128), 1)
    packed = jnp.where(lane == 0, sums[0], jnp.where(lane == 1, sums[1], sums[2]))
    packed = jnp.concatenate([packed, jnp.zeros((4, 128), F32)], axis=0)
    for b in range(BAND):
        out_ref[b] = packed


def roll_sources(source):
    vmem = pl.BlockSpec(memory_space=pltpu.VMEM)
    return pl.pallas_call(
        roll_kernel,
        out_shape=jax.ShapeDtypeStruct((HALF_CAPS * 6 * TGT, COLS), BF16),
        in_specs=[vmem],
        out_specs=vmem,
        scratch_shapes=[pltpu.VMEM((3, QUAD * 144, 128), F32)],
        compiler_params=pltpu.CompilerParams(vmem_limit_bytes=24 * 2**20),
        cost_estimate=pl.CostEstimate(flops=10**9, bytes_accessed=2**22, transcendentals=0),
        name="roll",
    )(source)


def per_device(positions, densities, operator, target_shift, weights):
    vmem = pl.BlockSpec(memory_space=pltpu.VMEM)
    smem = pl.BlockSpec(memory_space=pltpu.SMEM)
    lines = pl.pallas_call(
        pack_kernel,
        out_shape=jax.ShapeDtypeStruct((Z, LINES, 128), BF16),
        in_specs=[vmem],
        out_specs=vmem,
        scratch_shapes=[pltpu.VMEM((LINES, 128), F32)],
        compiler_params=pltpu.CompilerParams(vmem_limit_bytes=16 * 2**20),
        name="pack",
    )(operator)
    lines, positions, densities, target_shift, weights = lax.optimization_barrier(
        (lines, positions, densities, target_shift, weights)
    )
    lines = lax.all_to_all(lines, "z_half", 0, 0, tiled=True)
    weights = weights.reshape(Z, GROUPS, ROWS_HERE).transpose(1, 0, 2).reshape(GROUPS, NODES)
    source = jnp.concatenate([positions, densities], axis=1).reshape(144, LON)
    shifts = jnp.broadcast_to(target_shift.T[:, :, None], (TGT, 2, LON // 2)).reshape(TGT, LON)
    source = jnp.concatenate([source, shifts.astype(BF16)], axis=0)
    source = lax.all_gather(source[None], GROUP, axis=0, tiled=True)
    other = lax.ppermute(source, "z_low", [(0, 1), (1, 0)])
    mine = roll_sources(source)
    other = roll_sources(other)
    side = lax.axis_index("z_low").astype(jnp.int32)[None]
    parts, weights = pl.pallas_call(
        rotate_kernel,
        out_shape=(
            jax.ShapeDtypeStruct((GROUPS * BAND, 16, 128), F32),
            jax.ShapeDtypeStruct((GROUPS, NODES), F32),
        ),
        in_specs=[vmem] * 4 + [smem],
        out_specs=(vmem, vmem),
        scratch_shapes=[
            pltpu.VMEM((Z * LINES, 128), F32),
            pltpu.VMEM((NODES, COLS), BF16),
            pltpu.VMEM((PARITY, HALF_CAPS * 6 * TGT, NODES), F32),
        ],
        compiler_params=pltpu.CompilerParams(vmem_limit_bytes=32 * 2**20),
        name="rotate",
    )(mine, other, lines, weights, side)
    parts = lax.all_to_all(parts, ("z_low",) + GROUP + STRIP, 0, 0, tiled=True)
    found = pl.pallas_call(
        stokes_kernel,
        out_shape=jax.ShapeDtypeStruct((BAND, 8, 128), F32),
        in_specs=[vmem] * 2,
        out_specs=vmem,
        compiler_params=pltpu.CompilerParams(vmem_limit_bytes=32 * 2**20),
        name="stokes",
    )(parts.reshape(GROUPS, BAND, 16, 128), weights)
    found = lax.all_to_all(found, STRIP, 0, 0, tiled=True)
    return found[:, 0:4, 0:3].reshape(2, TGT, 3).transpose(0, 2, 1)


def solution(mesh):
    split = Mesh(mesh.devices.reshape(8, 2, 2, 2, 4, 2), CELL + STRIP)
    in_specs = (
        P(CELL, None, STRIP, None),
        P(CELL, None, STRIP, None),
        P(CELL, STRIP, None),
        P(CELL, None),
        P(),
    )
    return jax.shard_map(
        per_device, mesh=split, in_specs=in_specs, out_specs=P(CELL, None, None), check_vma=False
    )
```

```python
import jax
import jax.numpy as jnp
from jax import lax
from jax.experimental import pallas as pl
from jax.experimental.pallas import tpu as pltpu
from jax.sharding import Mesh
from jax.sharding import PartitionSpec as P

F32 = jnp.float32
BF16 = jnp.bfloat16

LAT_HERE = 12
LON = 192
COLS = LAT_HERE * LON
TGT = 16
ROWS_HERE = 10
Z = 8
QUAD = 4
PARITY = 2
BAND = 8
CAPS = 2 * QUAD
NODES = Z * ROWS_HERE
TILES = COLS // 128
LINES = ROWS_HERE * TILES
LEFT = 128 - NODES

CELL = ("z_half", "z_low", "y_hi", "core")
GROUP = ("y_hi", "core")
STRIP = ("x", "y_lo")

blob_radius = 0.5


def pack_kernel(op_ref, out_ref, lines):
    for r in range(ROWS_HERE):
        row = op_ref[r].astype(F32)
        high = row[:, 128:LON]
        at = r * TILES
        lines[at : at + LAT_HERE, :] = row[:, 0:128]
        lines[at + LAT_HERE : at + TILES, :] = jnp.concatenate([high[0:6], high[6:12]], axis=1)
    packed = lines[...].astype(BF16)
    for z in range(Z):
        out_ref[z] = packed


def roll_kernel(src_ref, rolled_ref, tiles):
    for p in range(QUAD):
        block = src_ref[p, 0:144, :].astype(F32)
        here = pl.ds(p * 144, 144)
        tiles[0, here, :] = block[:, 0:128]
        tiles[1, here, :] = jnp.concatenate([block[:, 128:192], block[:, 0:64]], axis=1)
        tiles[2, here, :] = block[:, 64:192]

    lane = lax.broadcasted_iota(jnp.int32, (TGT, 128), 1)

    def per_capsule(c, carry):
        column = src_ref[c // 2, 144:160, :].astype(F32)
        column = jnp.where(c % 2 == 0, column[:, 0:1], column[:, 96:97])
        shift = jnp.broadcast_to(column.astype(jnp.int32), (TGT, 128))
        take = jnp.bitwise_and(lane + shift, 127)
        goal = jnp.bitwise_and(lane - shift, 127)
        place = goal + shift
        early, late, low = place < 128, place < 256, goal < 64

        def rolled(value):
            return jnp.take_along_axis(value, take, axis=1, mode="promise_in_bounds").astype(BF16)

        for k in range(6):
            base = c * 72 + k * LAT_HERE
            to = pl.ds(pl.multiple_of((c * 6 + k) * TGT, TGT), TGT)

            def row(q, a):
                return jnp.broadcast_to(tiles[q, pl.ds(base + a, 1), :], (TGT, 128))

            for m in range(6):
                t = [row(q, m) for q in range(3)]
                u = [row(q, m + 6) for q in range(3)]
                first = jnp.where(early, t[0], jnp.where(late, t[1], t[2]))
                second = jnp.where(early, u[0], jnp.where(late, u[1], u[2]))
                high = jnp.where(
                    low,
                    jnp.where(early, t[1], t[2]),
                    jnp.where(early, u[2], jnp.where(late, u[0], u[1])),
                )
                rolled_ref[to, m * 128 : m * 128 + 128] = rolled(first)
                rolled_ref[to, (m + 6) * 128 : (m + 6) * 128 + 128] = rolled(second)
                rolled_ref[to, (m + 12) * 128 : (m + 12) * 128 + 128] = rolled(high)
        return carry

    lax.fori_loop(0, CAPS, per_capsule, 0)


def contract(rolled_ref, op_ref, lines, held, acc):
    for z in range(Z):
        lines[z * LINES : (z + 1) * LINES, :] = op_ref[z].astype(F32)
    for n in range(TILES):
        held[:, n * 128 : (n + 1) * 128] = lines[pl.ds(n, NODES, stride=TILES), :].astype(BF16)
    acc[...] = lax.dot_general(
        rolled_ref[...], held[...], (((1,), (1,)), ((), ())), preferred_element_type=F32
    )


def by_target(acc, store):
    upper = lax.broadcasted_iota(jnp.int32, (8, NODES), 0) < 4
    blank = jnp.zeros((8, 2 * 128 - 3 * NODES), F32)
    for c in range(CAPS):
        for half in range(2):
            found = [[], []]
            for pair in range(3):
                at = c * 96 + pair * 32 + half * 8
                one = acc[at : at + 8, :]
                two = acc[at + 16 : at + 24, :]
                found[0].append(jnp.where(upper, one, pltpu.roll(two, 4, 0)))
                found[1].append(jnp.where(upper, pltpu.roll(one, 4, 0), two))
            for j in range(2):
                a, b, d = found[j]
                store(
                    (c // 2) * BAND + (c % 2) * 4 + half * 2 + j,
                    jnp.concatenate([a, b[:, 0:LEFT]], axis=1),
                    jnp.concatenate([b[:, LEFT:NODES], d, blank], axis=1),
                )


def rotate_mine_kernel(rolled_ref, op_ref, out_ref, lines, held, acc):
    contract(rolled_ref, op_ref, lines, held, acc)

    def store(dest, one, two):
        out_ref[dest, 0:8, :] = one
        out_ref[dest, 8:16, :] = two

    by_target(acc, store)


def rotate_next_kernel(rolled_ref, op_ref, mine_ref, side_ref, out_ref, lines, held, acc):
    side = side_ref[0]
    out_ref[:, pl.ds(pl.multiple_of(side * 16, 16), 16), :] = mine_ref[...]
    contract(rolled_ref, op_ref, lines, held, acc)
    at = pl.multiple_of((1 - side) * 16, 16)

    def store(dest, one, two):
        out_ref[dest, pl.ds(at, 8), :] = one
        out_ref[dest, pl.ds(at + 8, 8), :] = two

    by_target(acc, store)


def stokes_kernel(parts_ref, weight_ref, out_ref):
    blob_sq = blob_radius * blob_radius
    pole = None
    sums = [jnp.zeros((4, 1), F32) for _ in range(3)]
    for n in range(QUAD * PARITY):
        g, rows_at = n // PARITY, (n % PARITY) * 16
        one = parts_ref[g, 0, rows_at : rows_at + 8, :]
        two = parts_ref[g, 0, rows_at + 8 : rows_at + 16, :]
        for b in range(1, BAND):
            one = one + parts_ref[g, b, rows_at : rows_at + 8, :]
            two = two + parts_ref[g, b, rows_at + 8 : rows_at + 16, :]
        rest = NODES - LEFT
        pairs = (
            one[:, 0:NODES],
            jnp.concatenate([one[:, NODES:128], two[:, 0:rest]], axis=1),
            two[:, rest : rest + NODES],
        )
        rows = [pairs[k // 2][4 * (k % 2) : 4 * (k % 2) + 4, :] for k in range(6)]
        if n == 0:
            pole = [rows[k][:, 0:1] for k in range(3)]
        weights = weight_ref[n : n + 1, :]
        d = [pole[k] - rows[k] for k in range(3)]
        f = rows[3:6]
        q = d[0] * d[0] + d[1] * d[1] + d[2] * d[2]
        along = d[0] * f[0] + d[1] * f[1] + d[2] * f[2]
        r = lax.rsqrt(q + blob_sq)
        kernel = weights * (r * r * r)
        near = (q + 2.0 * blob_sq) * kernel
        along = along * kernel
        for k in range(3):
            sums[k] = sums[k] + jnp.sum(near * f[k] + along * d[k], axis=1, keepdims=True)
    lane = lax.broadcasted_iota(jnp.int32, (4, 128), 1)
    packed = jnp.where(lane == 0, sums[0], jnp.where(lane == 1, sums[1], sums[2]))
    packed = jnp.concatenate([packed, jnp.zeros((4, 128), F32)], axis=0)
    for b in range(BAND):
        out_ref[b] = packed


def per_device(positions, densities, operator, target_shift, weights):
    vmem = pl.BlockSpec(memory_space=pltpu.VMEM)
    smem = pl.BlockSpec(memory_space=pltpu.SMEM)
    lines = pl.pallas_call(
        pack_kernel,
        out_shape=jax.ShapeDtypeStruct((Z, LINES, 128), BF16),
        in_specs=[vmem],
        out_specs=vmem,
        scratch_shapes=[pltpu.VMEM((LINES, 128), F32)],
        compiler_params=pltpu.CompilerParams(vmem_limit_bytes=16 * 2**20),
        name="pack",
    )(operator)
    lines, positions, densities, target_shift = lax.optimization_barrier(
        (lines, positions, densities, target_shift)
    )
    mine = lax.all_to_all(lines, "z_half", 0, 0, tiled=True)
    source = jnp.concatenate([positions, densities], axis=1).reshape(144, LON)
    shifts = jnp.broadcast_to(target_shift.T[:, :, None], (TGT, 2, LON // 2)).reshape(TGT, LON)
    source = jnp.concatenate([source, shifts.astype(BF16)], axis=0)
    source = lax.all_gather(source[None], GROUP, axis=0, tiled=True)
    mine, source = lax.optimization_barrier((mine, source))
    other = lax.ppermute(mine, "z_low", [(0, 1), (1, 0)])
    rolled = pl.pallas_call(
        roll_kernel,
        out_shape=jax.ShapeDtypeStruct((CAPS * 6 * TGT, COLS), BF16),
        in_specs=[vmem],
        out_specs=vmem,
        scratch_shapes=[pltpu.VMEM((3, QUAD * 144, 128), F32)],
        compiler_params=pltpu.CompilerParams(vmem_limit_bytes=24 * 2**20),
        cost_estimate=pl.CostEstimate(flops=10**9, bytes_accessed=2**22, transcendentals=0),
        name="roll",
    )(source)
    scratch = [
        pltpu.VMEM((Z * LINES, 128), F32),
        pltpu.VMEM((NODES, COLS), BF16),
        pltpu.VMEM((CAPS * 6 * TGT, NODES), F32),
    ]
    parts = pl.pallas_call(
        rotate_mine_kernel,
        out_shape=jax.ShapeDtypeStruct((QUAD * BAND, 16, 128), F32),
        in_specs=[vmem] * 2,
        out_specs=vmem,
        scratch_shapes=scratch,
        compiler_params=pltpu.CompilerParams(vmem_limit_bytes=24 * 2**20),
        cost_estimate=pl.CostEstimate(flops=10**9, bytes_accessed=2**22, transcendentals=0),
        name="rotate_mine",
    )(rolled, mine)
    side = lax.axis_index("z_low").astype(jnp.int32)[None]
    parts = pl.pallas_call(
        rotate_next_kernel,
        out_shape=jax.ShapeDtypeStruct((QUAD * BAND, 32, 128), F32),
        in_specs=[vmem] * 3 + [smem],
        out_specs=vmem,
        scratch_shapes=scratch,
        compiler_params=pltpu.CompilerParams(vmem_limit_bytes=24 * 2**20),
        name="rotate_next",
    )(rolled, other, parts, side)
    parts = lax.all_to_all(parts, GROUP + STRIP, 0, 0, tiled=True)
    weights = weights.reshape(Z, PARITY, QUAD, ROWS_HERE).transpose(2, 1, 0, 3)
    weights = weights.reshape(QUAD * PARITY, NODES)
    found = pl.pallas_call(
        stokes_kernel,
        out_shape=jax.ShapeDtypeStruct((BAND, 8, 128), F32),
        in_specs=[vmem] * 2,
        out_specs=vmem,
        compiler_params=pltpu.CompilerParams(vmem_limit_bytes=32 * 2**20),
        name="stokes",
    )(parts.reshape(QUAD, BAND, 32, 128), weights)
    found = lax.all_to_all(found, STRIP, 0, 0, tiled=True)
    return found[:, 0:4, 0:3].reshape(2, TGT, 3).transpose(0, 2, 1)


def solution(mesh):
    split = Mesh(mesh.devices.reshape(8, 2, 2, 2, 4, 2), CELL + STRIP)
    in_specs = (
        P(CELL, None, STRIP, None),
        P(CELL, None, STRIP, None),
        P(CELL, STRIP, None),
        P(CELL, None),
        P(),
    )
    return jax.shard_map(
        per_device, mesh=split, in_specs=in_specs, out_specs=P(CELL, None, None), check_vma=False
    )
```

```python
import jax
import jax.numpy as jnp
from jax import lax
from jax.experimental import pallas as pl
from jax.experimental.pallas import tpu as pltpu
from jax.sharding import Mesh
from jax.sharding import PartitionSpec as P

F32 = jnp.float32
BF16 = jnp.bfloat16

LAT_HERE = 12
LON = 192
COLS = LAT_HERE * LON
TGT = 16
ROWS_HERE = 10
Z = 8
GROUPS = 8
BAND = 8
CAPS = 2 * GROUPS
NODES = Z * ROWS_HERE
TILES = COLS // 128
LINES = ROWS_HERE * TILES
LEFT = 128 - NODES
HIGH_AT = 160
SOURCE_LINES = 240
HALF_ROWS = CAPS // 2 * 6 * TGT

CELL = ("z_half", "z_low", "y_hi", "core")
GROUP = ("z_low", "y_hi", "core")
STRIP = ("x", "y_lo")

blob_radius = 0.5


def pack_kernel(op_ref, out_ref, lines):
    for r in range(ROWS_HERE):
        row = op_ref[r].astype(F32)
        high = row[:, 128:LON]
        at = r * TILES
        lines[at : at + LAT_HERE, :] = row[:, 0:128]
        lines[at + LAT_HERE : at + TILES, :] = jnp.concatenate([high[0:6], high[6:12]], axis=1)
    packed = lines[...].astype(BF16)
    for z in range(Z):
        out_ref[z] = packed


def pack_source_kernel(source_ref, shift_ref, out_ref):
    rows = source_ref[...].astype(F32)
    out_ref[0:144, :] = rows[:, 0:128].astype(BF16)
    high = jnp.concatenate([rows[0:72, 128:LON], rows[72:144, 128:LON]], axis=1)
    high = jnp.concatenate([high, jnp.zeros((8, 128), F32)], axis=0)
    out_ref[HIGH_AT:SOURCE_LINES, :] = high.astype(BF16)
    same = lax.broadcasted_iota(jnp.int32, (TGT, TGT), 0) == lax.broadcasted_iota(
        jnp.int32, (TGT, TGT), 1
    )
    columns = []
    for i in range(2):
        shift = jnp.broadcast_to(shift_ref[i : i + 1, :].astype(F32), (TGT, TGT))
        column = jnp.sum(jnp.where(same, shift, 0.0), axis=1, keepdims=True)
        columns.append(jnp.broadcast_to(column, (TGT, 64)))
    out_ref[144:HIGH_AT, :] = jnp.concatenate(columns, axis=1).astype(BF16)


def roll_half(src_ref, half, rolled_ref, tiles):
    base_p = half * (GROUPS // 2)
    for p in range(GROUPS // 2):
        high = src_ref[base_p + p, HIGH_AT:SOURCE_LINES, :].astype(F32)[0:72, :]
        for i in range(2):
            here = pl.ds(p * 144 + i * 72, 72)
            low = src_ref[base_p + p, 0:144, :].astype(F32)[72 * i : 72 * i + 72, :]
            rest = high[:, 64 * i : 64 * i + 64]
            tiles[0, here, :] = low
            tiles[1, here, :] = jnp.concatenate([rest, low[:, 0:64]], axis=1)
            tiles[2, here, :] = jnp.concatenate([low[:, 64:128], rest], axis=1)

    lane = lax.broadcasted_iota(jnp.int32, (TGT, 128), 1)

    def per_capsule(c, carry):
        column = src_ref[base_p + c // 2, 144:HIGH_AT, :].astype(F32)
        column = jnp.where(c % 2 == 0, column[:, 0:1], column[:, 64:65])
        shift = jnp.broadcast_to(column.astype(jnp.int32), (TGT, 128))
        take = jnp.bitwise_and(lane + shift, 127)
        goal = jnp.bitwise_and(lane - shift, 127)
        place = goal + shift
        early, late, low = place < 128, place < 256, goal < 64

        def rolled(value):
            return jnp.take_along_axis(value, take, axis=1, mode="promise_in_bounds").astype(BF16)

        for k in range(6):
            base = c * 72 + k * LAT_HERE
            to = pl.ds(pl.multiple_of((c * 6 + k) * TGT, TGT), TGT)

            def row(q, a):
                return jnp.broadcast_to(tiles[q, pl.ds(base + a, 1), :], (TGT, 128))

            for m in range(6):
                t = [row(q, m) for q in range(3)]
                u = [row(q, m + 6) for q in range(3)]
                first = jnp.where(early, t[0], jnp.where(late, t[1], t[2]))
                second = jnp.where(early, u[0], jnp.where(late, u[1], u[2]))
                high = jnp.where(
                    low,
                    jnp.where(early, t[1], t[2]),
                    jnp.where(early, u[2], jnp.where(late, u[0], u[1])),
                )
                rolled_ref[to, m * 128 : m * 128 + 128] = rolled(first)
                rolled_ref[to, (m + 6) * 128 : (m + 6) * 128 + 128] = rolled(second)
                rolled_ref[to, (m + 12) * 128 : (m + 12) * 128 + 128] = rolled(high)
        return carry

    lax.fori_loop(0, CAPS // 2, per_capsule, 0)


def roll_kernel(src_ref, rolled_ref, tiles):
    roll_half(src_ref, 0, rolled_ref, tiles)


def rotate_kernel(src_ref, rolled_ref, op_ref, out_ref, tiles, rolled, lines, held, acc):
    roll_half(src_ref, 1, rolled, tiles)
    for z in range(Z):
        lines[z * LINES : (z + 1) * LINES, :] = op_ref[z].astype(F32)
    for n in range(TILES):
        held[:, n * 128 : (n + 1) * 128] = lines[pl.ds(n, NODES, stride=TILES), :].astype(BF16)
    for i, half_ref in enumerate((rolled_ref, rolled)):
        acc[i * HALF_ROWS : (i + 1) * HALF_ROWS, :] = lax.dot_general(
            half_ref[...], held[...], (((1,), (1,)), ((), ())), preferred_element_type=F32
        )
    upper = lax.broadcasted_iota(jnp.int32, (8, NODES), 0) < 4
    blank = jnp.zeros((8, 2 * 128 - 3 * NODES), F32)
    for c in range(CAPS):
        for half in range(2):
            found = [[], []]
            for pair in range(3):
                at = c * 96 + pair * 32 + half * 8
                one = acc[at : at + 8, :]
                two = acc[at + 16 : at + 24, :]
                found[0].append(jnp.where(upper, one, pltpu.roll(two, 4, 0)))
                found[1].append(jnp.where(upper, pltpu.roll(one, 4, 0), two))
            for j in range(2):
                dest = (c // 2) * BAND + (c % 2) * 4 + half * 2 + j
                a, b, d = found[j]
                out_ref[dest, 0:8, :] = jnp.concatenate([a, b[:, 0:LEFT]], axis=1)
                out_ref[dest, 8:16, :] = jnp.concatenate([b[:, LEFT:NODES], d, blank], axis=1)


def stokes_kernel(parts_ref, weight_ref, out_ref):
    blob_sq = blob_radius * blob_radius
    pole = None
    sums = [jnp.zeros((4, 1), F32) for _ in range(3)]
    for g in range(GROUPS):
        whole = parts_ref[g, 0]
        for b in range(1, BAND):
            whole = whole + parts_ref[g, b]
        one, two = whole[0:8, :], whole[8:16, :]
        rest = NODES - LEFT
        pairs = (
            one[:, 0:NODES],
            jnp.concatenate([one[:, NODES:128], two[:, 0:rest]], axis=1),
            two[:, rest : rest + NODES],
        )
        rows = [pairs[k // 2][4 * (k % 2) : 4 * (k % 2) + 4, :] for k in range(6)]
        if g == 0:
            pole = [rows[k][:, 0:1] for k in range(3)]
        weights = weight_ref[g : g + 1, :]
        d = [pole[k] - rows[k] for k in range(3)]
        f = rows[3:6]
        q = d[0] * d[0] + d[1] * d[1] + d[2] * d[2]
        along = d[0] * f[0] + d[1] * f[1] + d[2] * f[2]
        r = lax.rsqrt(q + blob_sq)
        kernel = weights * (r * r * r)
        near = (q + 2.0 * blob_sq) * kernel
        along = along * kernel
        for k in range(3):
            sums[k] = sums[k] + jnp.sum(near * f[k] + along * d[k], axis=1, keepdims=True)
    lane = lax.broadcasted_iota(jnp.int32, (4, 128), 1)
    packed = jnp.where(lane == 0, sums[0], jnp.where(lane == 1, sums[1], sums[2]))
    packed = jnp.concatenate([packed, jnp.zeros((4, 128), F32)], axis=0)
    for b in range(BAND):
        out_ref[b] = packed


def per_device(positions, densities, operator, target_shift, weights):
    vmem = pl.BlockSpec(memory_space=pltpu.VMEM)
    lines = pl.pallas_call(
        pack_kernel,
        out_shape=jax.ShapeDtypeStruct((Z, LINES, 128), BF16),
        in_specs=[vmem],
        out_specs=vmem,
        scratch_shapes=[pltpu.VMEM((LINES, 128), F32)],
        compiler_params=pltpu.CompilerParams(vmem_limit_bytes=16 * 2**20),
        name="pack",
    )(operator)
    lines, positions, densities, target_shift = lax.optimization_barrier(
        (lines, positions, densities, target_shift)
    )
    lines = lax.all_to_all(lines, "z_half", 0, 0, tiled=True)
    source = jnp.concatenate([positions, densities], axis=1).reshape(144, LON)
    source = pl.pallas_call(
        pack_source_kernel,
        out_shape=jax.ShapeDtypeStruct((SOURCE_LINES, 128), BF16),
        in_specs=[vmem] * 2,
        out_specs=vmem,
        compiler_params=pltpu.CompilerParams(vmem_limit_bytes=16 * 2**20),
        name="pack_source",
    )(source, target_shift)
    source = lax.all_gather(source[None], GROUP, axis=0, tiled=True)
    rolled = pl.pallas_call(
        roll_kernel,
        out_shape=jax.ShapeDtypeStruct((HALF_ROWS, COLS), BF16),
        in_specs=[vmem],
        out_specs=vmem,
        scratch_shapes=[pltpu.VMEM((3, GROUPS * 72, 128), F32)],
        compiler_params=pltpu.CompilerParams(vmem_limit_bytes=16 * 2**20),
        cost_estimate=pl.CostEstimate(flops=10**9, bytes_accessed=2**22, transcendentals=0),
        name="roll",
    )(source)
    parts = pl.pallas_call(
        rotate_kernel,
        out_shape=jax.ShapeDtypeStruct((GROUPS * BAND, 16, 128), F32),
        in_specs=[vmem] * 3,
        out_specs=vmem,
        scratch_shapes=[
            pltpu.VMEM((3, GROUPS * 72, 128), F32),
            pltpu.VMEM((HALF_ROWS, COLS), BF16),
            pltpu.VMEM((Z * LINES, 128), F32),
            pltpu.VMEM((NODES, COLS), BF16),
            pltpu.VMEM((CAPS * 6 * TGT, NODES), F32),
        ],
        compiler_params=pltpu.CompilerParams(vmem_limit_bytes=16 * 2**20),
        name="rotate",
    )(source, rolled, lines)
    parts = lax.all_to_all(parts, GROUP + STRIP, 0, 0, tiled=True)
    weights = weights.reshape(Z, GROUPS, ROWS_HERE).transpose(1, 0, 2).reshape(GROUPS, NODES)
    found = pl.pallas_call(
        stokes_kernel,
        out_shape=jax.ShapeDtypeStruct((BAND, 8, 128), F32),
        in_specs=[vmem] * 2,
        out_specs=vmem,
        compiler_params=pltpu.CompilerParams(vmem_limit_bytes=32 * 2**20),
        name="stokes",
    )(parts.reshape(GROUPS, BAND, 16, 128), weights)
    found = lax.all_to_all(found, STRIP, 0, 0, tiled=True)
    return found[:, 0:4, 0:3].reshape(2, TGT, 3).transpose(0, 2, 1)


def solution(mesh):
    split = Mesh(mesh.devices.reshape(8, 2, 2, 2, 4, 2), CELL + STRIP)
    in_specs = (
        P(CELL, None, STRIP, None),
        P(CELL, None, STRIP, None),
        P(CELL, STRIP, None),
        P(CELL, None),
        P(),
    )
    return jax.shard_map(
        per_device, mesh=split, in_specs=in_specs, out_specs=P(CELL, None, None), check_vma=False
    )
```

```python
import jax
import jax.numpy as jnp
from jax import lax
from jax.experimental import pallas as pl
from jax.experimental.pallas import tpu as pltpu
from jax.sharding import Mesh
from jax.sharding import PartitionSpec as P

F32 = jnp.float32
BF16 = jnp.bfloat16

LAT_HERE = 12
LON = 192
COLS = LAT_HERE * LON
TGT = 16
ROWS_HERE = 10
Z = 8
QUAD = 4
PARITY = 2
BAND = 8
CAPS = 2 * QUAD
NODES = Z * ROWS_HERE
TILES = COLS // 128
LINES = ROWS_HERE * TILES
LEFT = 128 - NODES

CELL = ("z_half", "z_low", "y_hi", "core")
GROUP = ("y_hi", "core")
STRIP = ("x", "y_lo")

blob_radius = 0.5


def pack_kernel(op_ref, out_ref, lines):
    for r in range(ROWS_HERE):
        row = op_ref[r].astype(F32)
        high = row[:, 128:LON]
        at = r * TILES
        lines[at : at + LAT_HERE, :] = row[:, 0:128]
        lines[at + LAT_HERE : at + TILES, :] = jnp.concatenate([high[0:6], high[6:12]], axis=1)
    packed = lines[...].astype(BF16)
    for z in range(Z):
        out_ref[z] = packed


def roll_kernel(src_ref, rolled_ref, tiles):
    for p in range(QUAD):
        block = src_ref[p, 0:144, :].astype(F32)
        here = pl.ds(p * 144, 144)
        tiles[0, here, :] = block[:, 0:128]
        tiles[1, here, :] = jnp.concatenate([block[:, 128:192], block[:, 0:64]], axis=1)
        tiles[2, here, :] = block[:, 64:192]

    lane = lax.broadcasted_iota(jnp.int32, (TGT, 128), 1)

    def per_capsule(c, carry):
        column = src_ref[c // 2, 144:160, :].astype(F32)
        column = jnp.where(c % 2 == 0, column[:, 0:1], column[:, 96:97])
        shift = jnp.broadcast_to(column.astype(jnp.int32), (TGT, 128))
        take = jnp.bitwise_and(lane + shift, 127)
        goal = jnp.bitwise_and(lane - shift, 127)
        place = goal + shift
        early, late, low = place < 128, place < 256, goal < 64

        def rolled(value):
            return jnp.take_along_axis(value, take, axis=1, mode="promise_in_bounds").astype(BF16)

        for k in range(6):
            base = c * 72 + k * LAT_HERE
            to = pl.ds(pl.multiple_of((c * 6 + k) * TGT, TGT), TGT)

            def row(q, a):
                return jnp.broadcast_to(tiles[q, pl.ds(base + a, 1), :], (TGT, 128))

            for m in range(6):
                t = [row(q, m) for q in range(3)]
                u = [row(q, m + 6) for q in range(3)]
                first = jnp.where(early, t[0], jnp.where(late, t[1], t[2]))
                second = jnp.where(early, u[0], jnp.where(late, u[1], u[2]))
                high = jnp.where(
                    low,
                    jnp.where(early, t[1], t[2]),
                    jnp.where(early, u[2], jnp.where(late, u[0], u[1])),
                )
                rolled_ref[to, m * 128 : m * 128 + 128] = rolled(first)
                rolled_ref[to, (m + 6) * 128 : (m + 6) * 128 + 128] = rolled(second)
                rolled_ref[to, (m + 12) * 128 : (m + 12) * 128 + 128] = rolled(high)
        return carry

    lax.fori_loop(0, CAPS, per_capsule, 0)


def contract(rolled_ref, op_ref, lines, held, acc):
    for z in range(Z):
        lines[z * LINES : (z + 1) * LINES, :] = op_ref[z].astype(F32)
    for n in range(TILES):
        held[:, n * 128 : (n + 1) * 128] = lines[pl.ds(n, NODES, stride=TILES), :].astype(BF16)
    acc[...] = lax.dot_general(
        rolled_ref[...], held[...], (((1,), (1,)), ((), ())), preferred_element_type=F32
    )


def by_target(acc, store):
    upper = lax.broadcasted_iota(jnp.int32, (8, NODES), 0) < 4
    blank = jnp.zeros((8, 2 * 128 - 3 * NODES), F32)
    for c in range(CAPS):
        for half in range(2):
            found = [[], []]
            for pair in range(3):
                at = c * 96 + pair * 32 + half * 8
                one = acc[at : at + 8, :]
                two = acc[at + 16 : at + 24, :]
                found[0].append(jnp.where(upper, one, pltpu.roll(two, 4, 0)))
                found[1].append(jnp.where(upper, pltpu.roll(one, 4, 0), two))
            for j in range(2):
                a, b, d = found[j]
                store(
                    (c // 2) * BAND + (c % 2) * 4 + half * 2 + j,
                    jnp.concatenate([a, b[:, 0:LEFT]], axis=1),
                    jnp.concatenate([b[:, LEFT:NODES], d, blank], axis=1),
                )


def rotate_mine_kernel(rolled_ref, op_ref, out_ref, lines, held, acc):
    contract(rolled_ref, op_ref, lines, held, acc)

    def store(dest, one, two):
        out_ref[dest, 0:8, :] = one
        out_ref[dest, 8:16, :] = two

    by_target(acc, store)


def rotate_next_kernel(
    rolled_ref, op_ref, mine_ref, weight_ref, side_ref, out_ref, weight_out_ref, lines, held, acc
):
    weight_out_ref[...] = weight_ref[...]
    side = side_ref[0]
    out_ref[:, pl.ds(pl.multiple_of(side * 16, 16), 16), :] = mine_ref[...]
    contract(rolled_ref, op_ref, lines, held, acc)
    at = pl.multiple_of((1 - side) * 16, 16)

    def store(dest, one, two):
        out_ref[dest, pl.ds(at, 8), :] = one
        out_ref[dest, pl.ds(at + 8, 8), :] = two

    by_target(acc, store)


def stokes_kernel(parts_ref, weight_ref, out_ref):
    blob_sq = blob_radius * blob_radius
    pole = None
    sums = [jnp.zeros((4, 1), F32) for _ in range(3)]
    for n in range(QUAD * PARITY):
        g, rows_at = n // PARITY, (n % PARITY) * 16
        one = parts_ref[g, 0, rows_at : rows_at + 8, :]
        two = parts_ref[g, 0, rows_at + 8 : rows_at + 16, :]
        for b in range(1, BAND):
            one = one + parts_ref[g, b, rows_at : rows_at + 8, :]
            two = two + parts_ref[g, b, rows_at + 8 : rows_at + 16, :]
        rest = NODES - LEFT
        pairs = (
            one[:, 0:NODES],
            jnp.concatenate([one[:, NODES:128], two[:, 0:rest]], axis=1),
            two[:, rest : rest + NODES],
        )
        rows = [pairs[k // 2][4 * (k % 2) : 4 * (k % 2) + 4, :] for k in range(6)]
        if n == 0:
            pole = [rows[k][:, 0:1] for k in range(3)]
        weights = weight_ref[n : n + 1, :]
        d = [pole[k] - rows[k] for k in range(3)]
        f = rows[3:6]
        q = d[0] * d[0] + d[1] * d[1] + d[2] * d[2]
        along = d[0] * f[0] + d[1] * f[1] + d[2] * f[2]
        r = lax.rsqrt(q + blob_sq)
        kernel = weights * (r * r * r)
        near = (q + 2.0 * blob_sq) * kernel
        along = along * kernel
        for k in range(3):
            sums[k] = sums[k] + jnp.sum(near * f[k] + along * d[k], axis=1, keepdims=True)
    lane = lax.broadcasted_iota(jnp.int32, (4, 128), 1)
    packed = jnp.where(lane == 0, sums[0], jnp.where(lane == 1, sums[1], sums[2]))
    packed = jnp.concatenate([packed, jnp.zeros((4, 128), F32)], axis=0)
    for b in range(BAND):
        out_ref[b] = packed


def swap_pairs():
    length = Z * PARITY
    pairs = []
    for z in range(length):
        for core in range(2):
            other = (z + 1 if (z + core) % 2 == 0 else z - 1) % length
            pairs.append((z * 2 + core, other * 2 + core))
    return pairs


def per_device(positions, densities, operator, target_shift, weights):
    vmem = pl.BlockSpec(memory_space=pltpu.VMEM)
    smem = pl.BlockSpec(memory_space=pltpu.SMEM)
    lines = pl.pallas_call(
        pack_kernel,
        out_shape=jax.ShapeDtypeStruct((Z, LINES, 128), BF16),
        in_specs=[vmem],
        out_specs=vmem,
        scratch_shapes=[pltpu.VMEM((LINES, 128), F32)],
        compiler_params=pltpu.CompilerParams(vmem_limit_bytes=16 * 2**20),
        name="pack",
    )(operator)
    lines, positions, densities, target_shift, weights = lax.optimization_barrier(
        (lines, positions, densities, target_shift, weights)
    )
    mine = lax.all_to_all(lines, "z_half", 0, 0, tiled=True)
    source = jnp.concatenate([positions, densities], axis=1).reshape(144, LON)
    shifts = jnp.broadcast_to(target_shift.T[:, :, None], (TGT, 2, LON // 2)).reshape(TGT, LON)
    source = jnp.concatenate([source, shifts.astype(BF16)], axis=0)
    source = lax.all_gather(source[None], GROUP, axis=0, tiled=True)
    rolled = pl.pallas_call(
        roll_kernel,
        out_shape=jax.ShapeDtypeStruct((CAPS * 6 * TGT, COLS), BF16),
        in_specs=[vmem],
        out_specs=vmem,
        scratch_shapes=[pltpu.VMEM((3, QUAD * 144, 128), F32)],
        compiler_params=pltpu.CompilerParams(vmem_limit_bytes=24 * 2**20),
        cost_estimate=pl.CostEstimate(flops=10**9, bytes_accessed=2**22, transcendentals=0),
        name="roll",
    )(source)
    weights = weights.reshape(Z, PARITY, QUAD, ROWS_HERE).transpose(2, 1, 0, 3)
    weights = weights.reshape(QUAD * PARITY, NODES)
    mine, rolled, weights = lax.optimization_barrier((mine, rolled, weights))
    other = lax.ppermute(mine, ("z_half", "z_low", "core"), swap_pairs())
    scratch = [
        pltpu.VMEM((Z * LINES, 128), F32),
        pltpu.VMEM((NODES, COLS), BF16),
        pltpu.VMEM((CAPS * 6 * TGT, NODES), F32),
    ]
    parts = pl.pallas_call(
        rotate_mine_kernel,
        out_shape=jax.ShapeDtypeStruct((QUAD * BAND, 16, 128), F32),
        in_specs=[vmem] * 2,
        out_specs=vmem,
        scratch_shapes=scratch,
        compiler_params=pltpu.CompilerParams(vmem_limit_bytes=24 * 2**20),
        cost_estimate=pl.CostEstimate(flops=10**9, bytes_accessed=2**22, transcendentals=0),
        name="rotate_mine",
    )(rolled, mine)
    side = lax.axis_index("z_low").astype(jnp.int32)[None]
    parts, weights = pl.pallas_call(
        rotate_next_kernel,
        out_shape=(
            jax.ShapeDtypeStruct((QUAD * BAND, 32, 128), F32),
            jax.ShapeDtypeStruct((QUAD * PARITY, NODES), F32),
        ),
        in_specs=[vmem] * 4 + [smem],
        out_specs=(vmem, vmem),
        scratch_shapes=scratch,
        compiler_params=pltpu.CompilerParams(vmem_limit_bytes=24 * 2**20),
        name="rotate_next",
    )(rolled, other, parts, weights, side)
    parts = lax.all_to_all(parts, GROUP + STRIP, 0, 0, tiled=True)
    found = pl.pallas_call(
        stokes_kernel,
        out_shape=jax.ShapeDtypeStruct((BAND, 8, 128), F32),
        in_specs=[vmem] * 2,
        out_specs=vmem,
        compiler_params=pltpu.CompilerParams(vmem_limit_bytes=32 * 2**20),
        name="stokes",
    )(parts.reshape(QUAD, BAND, 32, 128), weights)
    found = lax.all_to_all(found, STRIP, 0, 0, tiled=True)
    return found[:, 0:4, 0:3].reshape(2, TGT, 3).transpose(0, 2, 1)


def solution(mesh):
    split = Mesh(mesh.devices.reshape(8, 2, 2, 2, 4, 2), CELL + STRIP)
    in_specs = (
        P(CELL, None, STRIP, None),
        P(CELL, None, STRIP, None),
        P(CELL, STRIP, None),
        P(CELL, None),
        P(),
    )
    return jax.shard_map(
        per_device, mesh=split, in_specs=in_specs, out_specs=P(CELL, None, None), check_vma=False
    )
```

```python
import jax
import jax.numpy as jnp
from jax import lax
from jax.experimental import pallas as pl
from jax.experimental.pallas import tpu as pltpu
from jax.sharding import Mesh
from jax.sharding import PartitionSpec as P

F32 = jnp.float32
BF16 = jnp.bfloat16

LAT_HERE = 12
LON = 192
COLS = LAT_HERE * LON
TGT = 16
ROWS_HERE = 10
Z = 16
QUAD = 4
BAND = 8
CAPS = 2 * QUAD
NODES = Z * ROWS_HERE
TILES = COLS // 128
LINES = ROWS_HERE * TILES
HIGH_AT = 160
SOURCE_LINES = 240

CELL = ("z", "y_hi", "core")
GROUP = ("y_hi", "core")
STRIP = ("x", "y_lo")

blob_radius = 0.5


def pack_kernel(op_ref, source_ref, shift_ref, op_out_ref, source_out_ref, lines):
    for r in range(ROWS_HERE):
        row = op_ref[r].astype(F32)
        high = row[:, 128:LON]
        at = r * TILES
        lines[at : at + LAT_HERE, :] = row[:, 0:128]
        lines[at + LAT_HERE : at + TILES, :] = jnp.concatenate([high[0:6], high[6:12]], axis=1)
    op_out_ref[0] = lines[...].astype(BF16)
    rows = source_ref[...].astype(F32)
    low = rows[:, 0:128].astype(BF16)
    high = jnp.concatenate([rows[0:72, 128:LON], rows[72:144, 128:LON]], axis=1)
    high = jnp.concatenate([high, jnp.zeros((8, 128), F32)], axis=0).astype(BF16)
    same = lax.broadcasted_iota(jnp.int32, (TGT, TGT), 0) == lax.broadcasted_iota(
        jnp.int32, (TGT, TGT), 1
    )
    columns = []
    for i in range(2):
        shift = jnp.broadcast_to(shift_ref[i : i + 1, :].astype(F32), (TGT, TGT))
        column = jnp.sum(jnp.where(same, shift, 0.0), axis=1, keepdims=True)
        columns.append(jnp.broadcast_to(column, (TGT, 64)))
    columns = jnp.concatenate(columns, axis=1).astype(BF16)
    for p in range(QUAD):
        source_out_ref[p, 0:144, :] = low
        source_out_ref[p, 144:HIGH_AT, :] = columns
        source_out_ref[p, HIGH_AT:SOURCE_LINES, :] = high


def roll_kernel(src_ref, rolled_ref, tiles):
    for p in range(QUAD):
        high = src_ref[p, HIGH_AT:SOURCE_LINES, :].astype(F32)[0:72, :]
        for i in range(2):
            here = pl.ds(p * 144 + i * 72, 72)
            low = src_ref[p, 0:144, :].astype(F32)[72 * i : 72 * i + 72, :]
            rest = high[:, 64 * i : 64 * i + 64]
            tiles[0, here, :] = low
            tiles[1, here, :] = jnp.concatenate([rest, low[:, 0:64]], axis=1)
            tiles[2, here, :] = jnp.concatenate([low[:, 64:128], rest], axis=1)

    lane = lax.broadcasted_iota(jnp.int32, (TGT, 128), 1)

    def per_capsule(c, carry):
        column = src_ref[c // 2, 144:HIGH_AT, :].astype(F32)
        column = jnp.where(c % 2 == 0, column[:, 0:1], column[:, 64:65])
        shift = jnp.broadcast_to(column.astype(jnp.int32), (TGT, 128))
        take = jnp.bitwise_and(lane + shift, 127)
        goal = jnp.bitwise_and(lane - shift, 127)
        place = goal + shift
        early, late, low = place < 128, place < 256, goal < 64

        def rolled(value):
            return jnp.take_along_axis(value, take, axis=1, mode="promise_in_bounds").astype(BF16)

        for k in range(6):
            base = c * 72 + k * LAT_HERE
            to = pl.ds(pl.multiple_of((c * 6 + k) * TGT, TGT), TGT)

            def row(q, a):
                return jnp.broadcast_to(tiles[q, pl.ds(base + a, 1), :], (TGT, 128))

            for m in range(6):
                t = [row(q, m) for q in range(3)]
                u = [row(q, m + 6) for q in range(3)]
                first = jnp.where(early, t[0], jnp.where(late, t[1], t[2]))
                second = jnp.where(early, u[0], jnp.where(late, u[1], u[2]))
                high = jnp.where(
                    low,
                    jnp.where(early, t[1], t[2]),
                    jnp.where(early, u[2], jnp.where(late, u[0], u[1])),
                )
                rolled_ref[to, m * 128 : m * 128 + 128] = rolled(first)
                rolled_ref[to, (m + 6) * 128 : (m + 6) * 128 + 128] = rolled(second)
                rolled_ref[to, (m + 12) * 128 : (m + 12) * 128 + 128] = rolled(high)
        return carry

    lax.fori_loop(0, CAPS, per_capsule, 0)


def rotate_kernel(rolled_ref, op_ref, out_ref, lines, held, acc):
    for z in range(Z):
        lines[z * LINES : (z + 1) * LINES, :] = op_ref[z].astype(F32)
    for n in range(TILES):
        rows = lines[pl.ds(n, NODES, stride=TILES), :]
        held[:, n * 128 : (n + 1) * 128] = rows.astype(BF16)
    acc[...] = lax.dot_general(
        rolled_ref[...], held[...], (((1,), (1,)), ((), ())), preferred_element_type=F32
    )

    upper = lax.broadcasted_iota(jnp.int32, (8, NODES), 0) < 4
    for c in range(CAPS):
        for half in range(2):
            tails = [[], []]
            for pair in range(3):
                at = c * 96 + pair * 32 + half * 8
                one = acc[at : at + 8, :]
                two = acc[at + 16 : at + 24, :]
                lo = jnp.where(upper, one, pltpu.roll(two, 4, 0))
                hi = jnp.where(upper, pltpu.roll(one, 4, 0), two)
                for j, tile in enumerate((lo, hi)):
                    dest = (c // 2) * BAND + (c % 2) * 4 + half * 2 + j
                    out_ref[dest, pair * 8 : pair * 8 + 8, :] = tile[:, 0:128]
                    tails[j].append(tile[:, 128:NODES])
            for j in range(2):
                dest = (c // 2) * BAND + (c % 2) * 4 + half * 2 + j
                blank = jnp.zeros((8, 32), F32)
                out_ref[dest, 24:32, :] = jnp.concatenate([*tails[j], blank], axis=1)


def stokes_kernel(parts_ref, weight_ref, out_ref):
    blob_sq = blob_radius * blob_radius
    total = jnp.zeros((3, 4, 1), F32)
    pole = None
    sums = [jnp.zeros((4, 1), F32) for _ in range(3)]
    for g in range(QUAD):
        whole = parts_ref[g, 0]
        for b in range(1, BAND):
            whole = whole + parts_ref[g, b]
        main = [whole[4 * k : 4 * k + 4, :] for k in range(6)]
        tail = whole[24:32, :]
        rest = [
            tail[4 * (k % 2) : 4 * (k % 2) + 4, 32 * (k // 2) : 32 * (k // 2) + 32] for k in range(6)
        ]
        if g == 0:
            pole = [main[k][:, 0:1] for k in range(3)]
        for rows, weights in (
            (main, weight_ref[g : g + 1, 0:128]),
            (rest, weight_ref[g : g + 1, 128:NODES]),
        ):
            d = [pole[k] - rows[k] for k in range(3)]
            f = rows[3:6]
            q = d[0] * d[0] + d[1] * d[1] + d[2] * d[2]
            along = d[0] * f[0] + d[1] * f[1] + d[2] * f[2]
            s = q + blob_sq
            r = lax.rsqrt(s)
            kernel = weights * (r * r * r)
            near = (q + 2.0 * blob_sq) * kernel
            along = along * kernel
            for k in range(3):
                sums[k] = sums[k] + jnp.sum(near * f[k] + along * d[k], axis=1, keepdims=True)
    lane = lax.broadcasted_iota(jnp.int32, (4, 128), 1)
    packed = jnp.where(lane == 0, sums[0], jnp.where(lane == 1, sums[1], sums[2]))
    packed = jnp.concatenate([packed, jnp.zeros((4, 128), F32)], axis=0)
    for b in range(BAND):
        out_ref[b] = packed


def per_device(positions, densities, operator, target_shift, weights):
    vmem = pl.BlockSpec(memory_space=pltpu.VMEM)
    source = jnp.concatenate([positions, densities], axis=1).reshape(144, LON)
    lines, source = pl.pallas_call(
        pack_kernel,
        out_shape=(
            jax.ShapeDtypeStruct((1, LINES, 128), BF16),
            jax.ShapeDtypeStruct((QUAD, SOURCE_LINES, 128), BF16),
        ),
        in_specs=[vmem] * 3,
        out_specs=(vmem, vmem),
        scratch_shapes=[pltpu.VMEM((LINES, 128), F32)],
        compiler_params=pltpu.CompilerParams(vmem_limit_bytes=16 * 2**20),
        name="pack",
    )(operator, source, target_shift)
    source = lax.all_to_all(source, GROUP, 0, 0, tiled=True)
    lines = lax.all_gather(lines, "z", axis=0, tiled=True)
    rolled = pl.pallas_call(
        roll_kernel,
        out_shape=jax.ShapeDtypeStruct((CAPS * 6 * TGT, COLS), BF16),
        in_specs=[vmem],
        out_specs=vmem,
        scratch_shapes=[pltpu.VMEM((3, QUAD * 144, 128), F32)],
        compiler_params=pltpu.CompilerParams(vmem_limit_bytes=24 * 2**20),
        name="roll",
    )(source)
    parts = pl.pallas_call(
        rotate_kernel,
        out_shape=jax.ShapeDtypeStruct((QUAD * BAND, 32, 128), F32),
        in_specs=[vmem] * 2,
        out_specs=vmem,
        scratch_shapes=[
            pltpu.VMEM((Z * LINES, 128), F32),
            pltpu.VMEM((NODES, COLS), BF16),
            pltpu.VMEM((CAPS * 6 * TGT, NODES), F32),
        ],
        compiler_params=pltpu.CompilerParams(vmem_limit_bytes=24 * 2**20),
        name="rotate",
    )(rolled, lines)
    parts = lax.all_to_all(parts, GROUP + STRIP, 0, 0, tiled=True)
    weights = weights.reshape(Z, QUAD, ROWS_HERE).transpose(1, 0, 2).reshape(QUAD, NODES)
    found = pl.pallas_call(
        stokes_kernel,
        out_shape=jax.ShapeDtypeStruct((BAND, 8, 128), F32),
        in_specs=[vmem] * 2,
        out_specs=vmem,
        compiler_params=pltpu.CompilerParams(vmem_limit_bytes=32 * 2**20),
        name="stokes",
    )(parts.reshape(QUAD, BAND, 32, 128), weights)
    found = lax.all_to_all(found, STRIP, 0, 0, tiled=True)
    return found[:, 0:4, 0:3].reshape(2, TGT, 3).transpose(0, 2, 1)


def solution(mesh):
    split = Mesh(mesh.devices.reshape(16, 2, 2, 4, 2), CELL + STRIP)
    in_specs = (
        P(CELL, None, STRIP, None),
        P(CELL, None, STRIP, None),
        P(CELL, STRIP, None),
        P(CELL, None),
        P(),
    )
    return jax.shard_map(
        per_device, mesh=split, in_specs=in_specs, out_specs=P(CELL, None, None), check_vma=False
    )
```

```python
import jax
import jax.numpy as jnp
from jax import lax
from jax.experimental import pallas as pl
from jax.experimental.pallas import tpu as pltpu
from jax.sharding import Mesh
from jax.sharding import PartitionSpec as P

F32 = jnp.float32
BF16 = jnp.bfloat16

LAT_HERE = 12
LON = 192
COLS = LAT_HERE * LON
TGT = 16
ROWS_HERE = 10
Z = 16
SIDES = 2
BAND = 8
CAPS = 2 * SIDES
NODES = Z * ROWS_HERE
TILES = COLS // 128
LINES = ROWS_HERE * TILES
SENT_LINES = 184
HIGH_AT = 160
SOURCE_LINES = 240

CELL = ("z", "y_hi", "core")
STRIP = ("x", "y_lo")

blob_radius = 0.5


def pack_kernel(
    op_hbm, source_ref, shift_hbm, op_out_ref, source_out_ref, op_ref, shift_ref, lines, arrived
):
    copies = (
        pltpu.make_async_copy(shift_hbm, shift_ref, arrived.at[0]),
        pltpu.make_async_copy(op_hbm, op_ref, arrived.at[1]),
    )
    for copy in copies:
        copy.start()
    rows = source_ref[...].astype(F32)
    low = rows[:, 0:128].astype(BF16)
    high = jnp.concatenate([rows[0:72, 128:LON], rows[72:144, 128:LON]], axis=1)
    high = jnp.concatenate([high, jnp.zeros((8, 128), F32)], axis=0).astype(BF16)
    for p in range(SIDES):
        source_out_ref[p, 0:144, :] = low
        source_out_ref[p, HIGH_AT:SOURCE_LINES, :] = high
    copies[0].wait()
    same = lax.broadcasted_iota(jnp.int32, (TGT, TGT), 0) == lax.broadcasted_iota(
        jnp.int32, (TGT, TGT), 1
    )
    columns = []
    for i in range(2):
        shift = jnp.broadcast_to(shift_ref[i : i + 1, :].astype(F32), (TGT, TGT))
        column = jnp.sum(jnp.where(same, shift, 0.0), axis=1, keepdims=True)
        columns.append(jnp.broadcast_to(column, (TGT, 64)))
    for p in range(SIDES):
        source_out_ref[p, 144:HIGH_AT, :] = jnp.concatenate(columns, axis=1).astype(BF16)
    copies[1].wait()
    for r in range(ROWS_HERE):
        row = op_ref[r].astype(F32)
        high = row[:, 128:LON]
        at = r * TILES
        lines[at : at + LAT_HERE, :] = row[:, 0:128]
        lines[at + LAT_HERE : at + TILES, :] = jnp.concatenate([high[0:6], high[6:12]], axis=1)
    lines[LINES:SENT_LINES, :] = jnp.zeros((SENT_LINES - LINES, 128), F32)
    op_out_ref[0] = lines[...].astype(BF16)


def roll_kernel(src_ref, rolled_ref, tiles):
    for p in range(SIDES):
        high = src_ref[p, HIGH_AT:SOURCE_LINES, :].astype(F32)[0:72, :]
        for i in range(2):
            here = pl.ds(p * 144 + i * 72, 72)
            low = src_ref[p, 0:144, :].astype(F32)[72 * i : 72 * i + 72, :]
            rest = high[:, 64 * i : 64 * i + 64]
            tiles[0, here, :] = low
            tiles[1, here, :] = jnp.concatenate([rest, low[:, 0:64]], axis=1)
            tiles[2, here, :] = jnp.concatenate([low[:, 64:128], rest], axis=1)

    lane = lax.broadcasted_iota(jnp.int32, (TGT, 128), 1)

    def per_capsule(c, carry):
        column = src_ref[c // 2, 144:HIGH_AT, :].astype(F32)
        column = jnp.where(c % 2 == 0, column[:, 0:1], column[:, 64:65])
        shift = jnp.broadcast_to(column.astype(jnp.int32), (TGT, 128))
        take = jnp.bitwise_and(lane + shift, 127)
        goal = jnp.bitwise_and(lane - shift, 127)
        place = goal + shift
        early, late, low = place < 128, place < 256, goal < 64

        def rolled(value):
            return jnp.take_along_axis(value, take, axis=1, mode="promise_in_bounds").astype(BF16)

        for k in range(6):
            base = c * 72 + k * LAT_HERE
            to = pl.ds(pl.multiple_of((c * 6 + k) * TGT, TGT), TGT)

            def row(q, a):
                return jnp.broadcast_to(tiles[q, pl.ds(base + a, 1), :], (TGT, 128))

            for m in range(6):
                t = [row(q, m) for q in range(3)]
                u = [row(q, m + 6) for q in range(3)]
                first = jnp.where(early, t[0], jnp.where(late, t[1], t[2]))
                second = jnp.where(early, u[0], jnp.where(late, u[1], u[2]))
                high = jnp.where(
                    low,
                    jnp.where(early, t[1], t[2]),
                    jnp.where(early, u[2], jnp.where(late, u[0], u[1])),
                )
                rolled_ref[to, m * 128 : m * 128 + 128] = rolled(first)
                rolled_ref[to, (m + 6) * 128 : (m + 6) * 128 + 128] = rolled(second)
                rolled_ref[to, (m + 12) * 128 : (m + 12) * 128 + 128] = rolled(high)
        return carry

    lax.fori_loop(0, CAPS, per_capsule, 0)


def contract(rolled_ref, op_ref, lines, held, acc):
    for z in range(Z):
        lines[z * LINES : (z + 1) * LINES, :] = op_ref[z].astype(F32)[0:LINES, :]
    for n in range(TILES):
        held[:, n * 128 : (n + 1) * 128] = lines[pl.ds(n, NODES, stride=TILES), :].astype(BF16)
    acc[...] = lax.dot_general(
        rolled_ref[...], held[...], (((1,), (1,)), ((), ())), preferred_element_type=F32
    )


def by_target(acc, out_ref, at):
    upper = lax.broadcasted_iota(jnp.int32, (8, NODES), 0) < 4
    blank = jnp.zeros((8, 32), F32)
    for c in range(CAPS):
        first = (c // 2) * BAND + (c % 2) * 4
        for half in range(2):
            tails = [[], []]
            for pair in range(3):
                row = c * 96 + pair * 32 + half * 8
                one = acc[row : row + 8, :]
                two = acc[row + 16 : row + 24, :]
                lo = jnp.where(upper, one, pltpu.roll(two, 4, 0))
                hi = jnp.where(upper, pltpu.roll(one, 4, 0), two)
                for j, tile in enumerate((lo, hi)):
                    out_ref[first + half * 2 + j, pl.ds(at + pair * 8, 8), :] = tile[:, 0:128]
                    tails[j].append(tile[:, 128:NODES])
            for j in range(2):
                tail = jnp.concatenate([*tails[j], blank], axis=1)
                out_ref[first + half * 2 + j, pl.ds(at + 24, 8), :] = tail


def rotate_mine_kernel(rolled_ref, op_ref, out_ref, lines, held, acc):
    contract(rolled_ref, op_ref, lines, held, acc)
    by_target(acc, out_ref, 0)


def rotate_next_kernel(rolled_ref, op_ref, mine_ref, core_ref, out_ref, lines, held, acc):
    core = core_ref[0]
    out_ref[:, pl.ds(pl.multiple_of(core * 32, 32), 32), :] = mine_ref[...]
    contract(rolled_ref, op_ref, lines, held, acc)
    by_target(acc, out_ref, pl.multiple_of((1 - core) * 32, 32))


def stokes_kernel(parts_ref, weight_ref, out_ref):
    blob_sq = blob_radius * blob_radius
    total = jnp.zeros((3, 4, 1), F32)
    pole = None
    sums = [jnp.zeros((4, 1), F32) for _ in range(3)]
    for g in range(2 * SIDES):
        here = slice(32 * (g % 2), 32 * (g % 2) + 32)
        whole = parts_ref[g // 2, 0, here, :]
        for b in range(1, BAND):
            whole = whole + parts_ref[g // 2, b, here, :]
        main = [whole[4 * k : 4 * k + 4, :] for k in range(6)]
        tail = whole[24:32, :]
        rest = [
            tail[4 * (k % 2) : 4 * (k % 2) + 4, 32 * (k // 2) : 32 * (k // 2) + 32] for k in range(6)
        ]
        if g == 0:
            pole = [main[k][:, 0:1] for k in range(3)]
        for rows, weights in (
            (main, weight_ref[g : g + 1, 0:128]),
            (rest, weight_ref[g : g + 1, 128:NODES]),
        ):
            d = [pole[k] - rows[k] for k in range(3)]
            f = rows[3:6]
            q = d[0] * d[0] + d[1] * d[1] + d[2] * d[2]
            along = d[0] * f[0] + d[1] * f[1] + d[2] * f[2]
            s = q + blob_sq
            r = lax.rsqrt(s)
            kernel = weights * (r * r * r)
            near = (q + 2.0 * blob_sq) * kernel
            along = along * kernel
            for k in range(3):
                sums[k] = sums[k] + jnp.sum(near * f[k] + along * d[k], axis=1, keepdims=True)
    lane = lax.broadcasted_iota(jnp.int32, (4, 128), 1)
    packed = jnp.where(lane == 0, sums[0], jnp.where(lane == 1, sums[1], sums[2]))
    packed = jnp.concatenate([packed, jnp.zeros((4, 128), F32)], axis=0)
    for b in range(BAND):
        out_ref[b] = packed


def per_device(positions, densities, operator, target_shift, weights):
    vmem = pl.BlockSpec(memory_space=pltpu.VMEM)
    smem = pl.BlockSpec(memory_space=pltpu.SMEM)
    hbm = pl.BlockSpec(memory_space=pl.ANY)
    source = jnp.concatenate([positions, densities], axis=1).reshape(144, LON)
    lines, source = pl.pallas_call(
        pack_kernel,
        out_shape=(
            jax.ShapeDtypeStruct((1, SENT_LINES, 128), BF16),
            jax.ShapeDtypeStruct((SIDES, SOURCE_LINES, 128), BF16),
        ),
        in_specs=[hbm, vmem, hbm],
        out_specs=(vmem, vmem),
        scratch_shapes=[
            pltpu.VMEM((ROWS_HERE, LAT_HERE, LON), BF16),
            pltpu.VMEM((2, TGT), jnp.int32),
            pltpu.VMEM((SENT_LINES, 128), F32),
            pltpu.SemaphoreType.DMA((2,)),
        ],
        compiler_params=pltpu.CompilerParams(vmem_limit_bytes=60 * 2**20),
        name="pack",
    )(operator, source, target_shift)
    source = lax.all_to_all(source, "y_hi", 0, 0, tiled=True)
    mine = lax.all_gather(lines, "z", axis=0, tiled=True)
    mine, source = lax.optimization_barrier((mine, source))
    other = lax.ppermute(mine, "core", [(0, 1), (1, 0)])
    rolled = pl.pallas_call(
        roll_kernel,
        out_shape=jax.ShapeDtypeStruct((CAPS * 6 * TGT, COLS), BF16),
        in_specs=[vmem],
        out_specs=vmem,
        scratch_shapes=[pltpu.VMEM((3, SIDES * 144, 128), F32)],
        compiler_params=pltpu.CompilerParams(vmem_limit_bytes=16 * 2**20),
        cost_estimate=pl.CostEstimate(flops=10**9, bytes_accessed=2**22, transcendentals=0),
        name="roll",
    )(source)
    scratch = [
        pltpu.VMEM((Z * LINES, 128), F32),
        pltpu.VMEM((NODES, COLS), BF16),
        pltpu.VMEM((CAPS * 6 * TGT, NODES), F32),
    ]
    core = lax.axis_index("core").astype(jnp.int32)[None]
    parts = pl.pallas_call(
        rotate_mine_kernel,
        out_shape=jax.ShapeDtypeStruct((SIDES * BAND, 32, 128), F32),
        in_specs=[vmem] * 2,
        out_specs=vmem,
        scratch_shapes=scratch,
        compiler_params=pltpu.CompilerParams(vmem_limit_bytes=16 * 2**20),
        cost_estimate=pl.CostEstimate(flops=10**9, bytes_accessed=2**22, transcendentals=0),
        name="rotate_mine",
    )(rolled, mine)
    parts = pl.pallas_call(
        rotate_next_kernel,
        out_shape=jax.ShapeDtypeStruct((SIDES * BAND, 64, 128), F32),
        in_specs=[vmem] * 3 + [smem],
        out_specs=vmem,
        scratch_shapes=scratch,
        compiler_params=pltpu.CompilerParams(vmem_limit_bytes=16 * 2**20),
        name="rotate_next",
    )(rolled, other, parts, core)
    parts = lax.all_to_all(parts, ("y_hi",) + STRIP, 0, 0, tiled=True)
    weights = weights.reshape(Z, 2 * SIDES, ROWS_HERE).transpose(1, 0, 2)
    weights = weights.reshape(2 * SIDES, NODES)
    found = pl.pallas_call(
        stokes_kernel,
        out_shape=jax.ShapeDtypeStruct((BAND, 8, 128), F32),
        in_specs=[vmem] * 2,
        out_specs=vmem,
        compiler_params=pltpu.CompilerParams(vmem_limit_bytes=16 * 2**20),
        name="stokes",
    )(parts.reshape(SIDES, BAND, 64, 128), weights)
    found = lax.all_to_all(found, STRIP, 0, 0, tiled=True)
    return found[:, 0:4, 0:3].reshape(2, TGT, 3).transpose(0, 2, 1)


def solution(mesh):
    split = Mesh(mesh.devices.reshape(16, 2, 2, 4, 2), CELL + STRIP)
    in_specs = (
        P(CELL, None, STRIP, None),
        P(CELL, None, STRIP, None),
        P(CELL, STRIP, None),
        P(CELL, None),
        P(),
    )
    return jax.shard_map(
        per_device, mesh=split, in_specs=in_specs, out_specs=P(CELL, None, None), check_vma=False
    )
```

```python
import jax
import jax.numpy as jnp
from jax import lax
from jax.experimental import pallas as pl
from jax.experimental.pallas import tpu as pltpu
from jax.sharding import Mesh
from jax.sharding import PartitionSpec as P

F32 = jnp.float32
BF16 = jnp.bfloat16

LAT_HERE = 12
LON = 192
COLS = LAT_HERE * LON
TGT = 16
ROWS_HERE = 10
Z = 8
GROUPS = 8
BAND = 8
CAPS = 2 * GROUPS
NODES = Z * ROWS_HERE
TILES = COLS // 128
LINES = ROWS_HERE * TILES
LEFT = 128 - NODES
HIGH_AT = 160
SOURCE_LINES = 240
STEPS = 4
STEP_CAPS = CAPS // STEPS
STEP_ROWS = STEP_CAPS * 6 * TGT

CELL = ("z_half", "z_low", "y_hi", "core")
GROUP = ("y_hi", "core")
STRIP = ("x", "y_lo")

blob_radius = 0.5


def pack_kernel(op_ref, op_out_ref, lines):
    for r in range(ROWS_HERE):
        row = op_ref[r].astype(F32)
        high = row[:, 128:LON]
        at = r * TILES
        lines[at : at + LAT_HERE, :] = row[:, 0:128]
        lines[at + LAT_HERE : at + TILES, :] = jnp.concatenate([high[0:6], high[6:12]], axis=1)
    packed = lines[...].astype(BF16)
    for z in range(Z):
        op_out_ref[z] = packed


def pack_source_kernel(source_ref, shift_ref, source_out_ref):
    rows = source_ref[...].astype(F32)
    low = rows[:, 0:128].astype(BF16)
    high = jnp.concatenate([rows[0:72, 128:LON], rows[72:144, 128:LON]], axis=1)
    high = jnp.concatenate([high, jnp.zeros((8, 128), F32)], axis=0).astype(BF16)
    same = lax.broadcasted_iota(jnp.int32, (TGT, TGT), 0) == lax.broadcasted_iota(
        jnp.int32, (TGT, TGT), 1
    )
    columns = []
    for i in range(2):
        shift = jnp.broadcast_to(shift_ref[i : i + 1, :].astype(F32), (TGT, TGT))
        column = jnp.sum(jnp.where(same, shift, 0.0), axis=1, keepdims=True)
        columns.append(jnp.broadcast_to(column, (TGT, 64)))
    columns = jnp.concatenate(columns, axis=1).astype(BF16)
    source_out_ref[0:144, :] = low
    source_out_ref[144:HIGH_AT, :] = columns
    source_out_ref[HIGH_AT:SOURCE_LINES, :] = high


def roll_kernel(src_ref, rolled_ref, tiles):
    for p in range(2):
        high = src_ref[p, 0, HIGH_AT:SOURCE_LINES, :].astype(F32)[0:72, :]
        for i in range(2):
            here = pl.ds(p * 144 + i * 72, 72)
            low = src_ref[p, 0, 0:144, :].astype(F32)[72 * i : 72 * i + 72, :]
            rest = high[:, 64 * i : 64 * i + 64]
            tiles[0, here, :] = low
            tiles[1, here, :] = jnp.concatenate([rest, low[:, 0:64]], axis=1)
            tiles[2, here, :] = jnp.concatenate([low[:, 64:128], rest], axis=1)

    lane = lax.broadcasted_iota(jnp.int32, (TGT, 128), 1)

    def per_capsule(c, carry):
        column = src_ref[c // 2, 0, 144:HIGH_AT, :].astype(F32)
        column = jnp.where(c % 2 == 0, column[:, 0:1], column[:, 64:65])
        shift = jnp.broadcast_to(column.astype(jnp.int32), (TGT, 128))
        take = jnp.bitwise_and(lane + shift, 127)
        goal = jnp.bitwise_and(lane - shift, 127)
        place = goal + shift
        early, late, low = place < 128, place < 256, goal < 64

        def rolled(value):
            return jnp.take_along_axis(value, take, axis=1, mode="promise_in_bounds").astype(BF16)

        for k in range(6):
            base = c * 72 + k * LAT_HERE
            to = pl.ds(pl.multiple_of((c * 6 + k) * TGT, TGT), TGT)

            def row(q, a):
                return jnp.broadcast_to(tiles[q, pl.ds(base + a, 1), :], (TGT, 128))

            for m in range(6):
                t = [row(q, m) for q in range(3)]
                u = [row(q, m + 6) for q in range(3)]
                first = jnp.where(early, t[0], jnp.where(late, t[1], t[2]))
                second = jnp.where(early, u[0], jnp.where(late, u[1], u[2]))
                high = jnp.where(
                    low,
                    jnp.where(early, t[1], t[2]),
                    jnp.where(early, u[2], jnp.where(late, u[0], u[1])),
                )
                rolled_ref[to, m * 128 : m * 128 + 128] = rolled(first)
                rolled_ref[to, (m + 6) * 128 : (m + 6) * 128 + 128] = rolled(second)
                rolled_ref[to, (m + 12) * 128 : (m + 12) * 128 + 128] = rolled(high)
        return carry

    lax.fori_loop(0, STEP_CAPS, per_capsule, 0)


def rotate_kernel(rolled_ref, op_ref, out_ref, lines, held, acc):
    @pl.when(pl.program_id(0) == 0)
    def _():
        for z in range(Z):
            lines[z * LINES : (z + 1) * LINES, :] = op_ref[z].astype(F32)
        for n in range(TILES):
            held[:, n * 128 : (n + 1) * 128] = lines[pl.ds(n, NODES, stride=TILES), :].astype(BF16)

    acc[...] = lax.dot_general(
        rolled_ref[...], held[...], (((1,), (1,)), ((), ())), preferred_element_type=F32
    )
    upper = lax.broadcasted_iota(jnp.int32, (8, NODES), 0) < 4
    blank = jnp.zeros((8, 2 * 128 - 3 * NODES), F32)
    for c in range(STEP_CAPS):
        for half in range(2):
            found = [[], []]
            for pair in range(3):
                at = c * 96 + pair * 32 + half * 8
                one = acc[at : at + 8, :]
                two = acc[at + 16 : at + 24, :]
                found[0].append(jnp.where(upper, one, pltpu.roll(two, 4, 0)))
                found[1].append(jnp.where(upper, pltpu.roll(one, 4, 0), two))
            for j in range(2):
                dest = (c // 2) * BAND + (c % 2) * 4 + half * 2 + j
                a, b, d = found[j]
                out_ref[dest, 0:8, :] = jnp.concatenate([a, b[:, 0:LEFT]], axis=1)
                out_ref[dest, 8:16, :] = jnp.concatenate([b[:, LEFT:NODES], d, blank], axis=1)


def stokes_kernel(parts_ref, weight_ref, out_ref):
    blob_sq = blob_radius * blob_radius
    pole = None
    sums = [jnp.zeros((4, 1), F32) for _ in range(3)]
    for g in range(GROUPS):
        whole = parts_ref[g, 0]
        for b in range(1, BAND):
            whole = whole + parts_ref[g, b]
        one, two = whole[0:8, :], whole[8:16, :]
        rest = NODES - LEFT
        pairs = (
            one[:, 0:NODES],
            jnp.concatenate([one[:, NODES:128], two[:, 0:rest]], axis=1),
            two[:, rest : rest + NODES],
        )
        rows = [pairs[k // 2][4 * (k % 2) : 4 * (k % 2) + 4, :] for k in range(6)]
        if g == 0:
            pole = [rows[k][:, 0:1] for k in range(3)]
        weights = weight_ref[g : g + 1, :]
        d = [pole[k] - rows[k] for k in range(3)]
        f = rows[3:6]
        q = d[0] * d[0] + d[1] * d[1] + d[2] * d[2]
        along = d[0] * f[0] + d[1] * f[1] + d[2] * f[2]
        r = lax.rsqrt(q + blob_sq)
        kernel = weights * (r * r * r)
        near = (q + 2.0 * blob_sq) * kernel
        along = along * kernel
        for k in range(3):
            sums[k] = sums[k] + jnp.sum(near * f[k] + along * d[k], axis=1, keepdims=True)
    lane = lax.broadcasted_iota(jnp.int32, (4, 128), 1)
    packed = jnp.where(lane == 0, sums[0], jnp.where(lane == 1, sums[1], sums[2]))
    packed = jnp.concatenate([packed, jnp.zeros((4, 128), F32)], axis=0)
    for b in range(BAND):
        out_ref[b] = packed


def per_device(positions, densities, operator, target_shift, weights):
    vmem = pl.BlockSpec(memory_space=pltpu.VMEM)
    source = jnp.concatenate([positions, densities], axis=1).reshape(144, LON)
    source = pl.pallas_call(
        pack_source_kernel,
        out_shape=jax.ShapeDtypeStruct((SOURCE_LINES, 128), BF16),
        in_specs=[vmem] * 2,
        out_specs=vmem,
        compiler_params=pltpu.CompilerParams(vmem_limit_bytes=16 * 2**20),
        name="pack_source",
    )(source, target_shift)
    operator, source = lax.optimization_barrier((operator, source))
    other = lax.ppermute(source, "z_low", [(0, 1), (1, 0)])
    lines = pl.pallas_call(
        pack_kernel,
        out_shape=jax.ShapeDtypeStruct((Z, LINES, 128), BF16),
        in_specs=[vmem],
        out_specs=vmem,
        scratch_shapes=[pltpu.VMEM((LINES, 128), F32)],
        compiler_params=pltpu.CompilerParams(vmem_limit_bytes=16 * 2**20),
        cost_estimate=pl.CostEstimate(flops=2 * 10**10, bytes_accessed=2**25, transcendentals=0),
        name="pack",
    )(operator)
    lines, other = lax.optimization_barrier((lines, other))
    lines = lax.all_to_all(lines, "z_half", 0, 0, tiled=True)
    even = lax.axis_index("z_low") == 0
    source = jnp.stack([jnp.where(even, source, other), jnp.where(even, other, source)])
    source = lax.all_gather(source[None], GROUP, axis=0, tiled=True)
    rolled = pl.pallas_call(
        roll_kernel,
        grid=(STEPS,),
        out_shape=jax.ShapeDtypeStruct((CAPS * 6 * TGT, COLS), BF16),
        in_specs=[pl.BlockSpec((2, 1, SOURCE_LINES, 128), lambda n: (n % 2, n // 2, 0, 0))],
        out_specs=pl.BlockSpec((STEP_ROWS, COLS), lambda n: (n, 0)),
        scratch_shapes=[pltpu.VMEM((3, 2 * 144, 128), F32)],
        compiler_params=pltpu.CompilerParams(vmem_limit_bytes=60 * 2**20),
        cost_estimate=pl.CostEstimate(flops=10**9, bytes_accessed=2**22, transcendentals=0),
        name="roll",
    )(source)
    parts = pl.pallas_call(
        rotate_kernel,
        grid=(STEPS,),
        out_shape=jax.ShapeDtypeStruct((GROUPS * BAND, 16, 128), F32),
        in_specs=[
            pl.BlockSpec((STEP_ROWS, COLS), lambda n: (n, 0)),
            pl.BlockSpec((Z, LINES, 128), lambda n: (0, 0, 0)),
        ],
        out_specs=pl.BlockSpec((GROUPS * BAND // STEPS, 16, 128), lambda n: (n, 0, 0)),
        scratch_shapes=[
            pltpu.VMEM((Z * LINES, 128), F32),
            pltpu.VMEM((NODES, COLS), BF16),
            pltpu.VMEM((STEP_ROWS, NODES), F32),
        ],
        compiler_params=pltpu.CompilerParams(vmem_limit_bytes=54 * 2**20),
        name="rotate",
    )(rolled, lines)
    parts = lax.all_to_all(parts, ("z_low",) + GROUP + STRIP, 0, 0, tiled=True)
    weights = weights.reshape(Z, GROUPS, ROWS_HERE).transpose(1, 0, 2).reshape(GROUPS, NODES)
    found = pl.pallas_call(
        stokes_kernel,
        out_shape=jax.ShapeDtypeStruct((BAND, 8, 128), F32),
        in_specs=[vmem] * 2,
        out_specs=vmem,
        compiler_params=pltpu.CompilerParams(vmem_limit_bytes=32 * 2**20),
        name="stokes",
    )(parts.reshape(GROUPS, BAND, 16, 128), weights)
    found = lax.all_to_all(found, STRIP, 0, 0, tiled=True)
    return found[:, 0:4, 0:3].reshape(2, TGT, 3).transpose(0, 2, 1)


def solution(mesh):
    split = Mesh(mesh.devices.reshape(8, 2, 2, 2, 4, 2), CELL + STRIP)
    in_specs = (
        P(CELL, None, STRIP, None),
        P(CELL, None, STRIP, None),
        P(CELL, STRIP, None),
        P(CELL, None),
        P(),
    )
    return jax.shard_map(
        per_device, mesh=split, in_specs=in_specs, out_specs=P(CELL, None, None), check_vma=False
    )
```

```python
import jax
import jax.numpy as jnp
from jax import lax
from jax.experimental import pallas as pl
from jax.experimental.pallas import tpu as pltpu
from jax.sharding import Mesh
from jax.sharding import PartitionSpec as P

F32 = jnp.float32
BF16 = jnp.bfloat16

LAT_HERE = 12
LON = 192
COLS = LAT_HERE * LON
TGT = 16
ROWS_HERE = 10
Z = 16
SIDES = 2
BAND = 8
CAPS = 2 * SIDES
NODES = Z * ROWS_HERE
TILES = COLS // 128
LINES = ROWS_HERE * TILES
SENT_LINES = 184
HIGH_AT = 160
SOURCE_LINES = 240

CELL = ("z", "y_hi", "core")
STRIP = ("x", "y_lo")

blob_radius = 0.5


def pack_kernel(op_ref, source_ref, shift_ref, op_out_ref, source_out_ref, lines):
    for r in range(ROWS_HERE):
        row = op_ref[r].astype(F32)
        high = row[:, 128:LON]
        at = r * TILES
        lines[at : at + LAT_HERE, :] = row[:, 0:128]
        lines[at + LAT_HERE : at + TILES, :] = jnp.concatenate([high[0:6], high[6:12]], axis=1)
    lines[LINES:SENT_LINES, :] = jnp.zeros((SENT_LINES - LINES, 128), F32)
    op_out_ref[0] = lines[...].astype(BF16)
    rows = source_ref[...].astype(F32)
    low = rows[:, 0:128].astype(BF16)
    high = jnp.concatenate([rows[0:72, 128:LON], rows[72:144, 128:LON]], axis=1)
    high = jnp.concatenate([high, jnp.zeros((8, 128), F32)], axis=0).astype(BF16)
    same = lax.broadcasted_iota(jnp.int32, (TGT, TGT), 0) == lax.broadcasted_iota(
        jnp.int32, (TGT, TGT), 1
    )
    columns = []
    for i in range(2):
        shift = jnp.broadcast_to(shift_ref[i : i + 1, :].astype(F32), (TGT, TGT))
        column = jnp.sum(jnp.where(same, shift, 0.0), axis=1, keepdims=True)
        columns.append(jnp.broadcast_to(column, (TGT, 64)))
    columns = jnp.concatenate(columns, axis=1).astype(BF16)
    source_out_ref[0:144, :] = low
    source_out_ref[144:HIGH_AT, :] = columns
    source_out_ref[HIGH_AT:SOURCE_LINES, :] = high


def roll_kernel(mine_ref, next_ref, rolled_ref, tiles):
    for p, src_ref in enumerate((mine_ref, next_ref)):
        high = src_ref[HIGH_AT:SOURCE_LINES, :].astype(F32)[0:72, :]
        for i in range(2):
            here = pl.ds(p * 144 + i * 72, 72)
            low = src_ref[0:144, :].astype(F32)[72 * i : 72 * i + 72, :]
            rest = high[:, 64 * i : 64 * i + 64]
            tiles[0, here, :] = low
            tiles[1, here, :] = jnp.concatenate([rest, low[:, 0:64]], axis=1)
            tiles[2, here, :] = jnp.concatenate([low[:, 64:128], rest], axis=1)

    lane = lax.broadcasted_iota(jnp.int32, (TGT, 128), 1)

    def per_capsule(c, carry):
        column = jnp.where(c // 2 == 0, mine_ref[144:HIGH_AT, :], next_ref[144:HIGH_AT, :]).astype(F32)
        column = jnp.where(c % 2 == 0, column[:, 0:1], column[:, 64:65])
        shift = jnp.broadcast_to(column.astype(jnp.int32), (TGT, 128))
        take = jnp.bitwise_and(lane + shift, 127)
        goal = jnp.bitwise_and(lane - shift, 127)
        place = goal + shift
        early, late, low = place < 128, place < 256, goal < 64

        def rolled(value):
            return jnp.take_along_axis(value, take, axis=1, mode="promise_in_bounds").astype(BF16)

        for k in range(6):
            base = c * 72 + k * LAT_HERE
            to = pl.ds(pl.multiple_of((c * 6 + k) * TGT, TGT), TGT)

            def row(q, a):
                return jnp.broadcast_to(tiles[q, pl.ds(base + a, 1), :], (TGT, 128))

            for m in range(6):
                t = [row(q, m) for q in range(3)]
                u = [row(q, m + 6) for q in range(3)]
                first = jnp.where(early, t[0], jnp.where(late, t[1], t[2]))
                second = jnp.where(early, u[0], jnp.where(late, u[1], u[2]))
                high = jnp.where(
                    low,
                    jnp.where(early, t[1], t[2]),
                    jnp.where(early, u[2], jnp.where(late, u[0], u[1])),
                )
                rolled_ref[to, m * 128 : m * 128 + 128] = rolled(first)
                rolled_ref[to, (m + 6) * 128 : (m + 6) * 128 + 128] = rolled(second)
                rolled_ref[to, (m + 12) * 128 : (m + 12) * 128 + 128] = rolled(high)
        return carry

    lax.fori_loop(0, CAPS, per_capsule, 0)


def contract(rolled_ref, op_ref, lines, held, acc):
    for z in range(Z):
        lines[z * LINES : (z + 1) * LINES, :] = op_ref[z].astype(F32)[0:LINES, :]
    for n in range(TILES):
        held[:, n * 128 : (n + 1) * 128] = lines[pl.ds(n, NODES, stride=TILES), :].astype(BF16)
    acc[...] = lax.dot_general(
        rolled_ref[...], held[...], (((1,), (1,)), ((), ())), preferred_element_type=F32
    )


def by_target(acc, side, out_ref, at):
    upper = lax.broadcasted_iota(jnp.int32, (8, NODES), 0) < 4
    blank = jnp.zeros((8, 32), F32)
    for c in range(CAPS):
        first = jnp.bitwise_xor(side, c // 2) * BAND + (c % 2) * 4
        for half in range(2):
            tails = [[], []]
            for pair in range(3):
                row = c * 96 + pair * 32 + half * 8
                one = acc[row : row + 8, :]
                two = acc[row + 16 : row + 24, :]
                lo = jnp.where(upper, one, pltpu.roll(two, 4, 0))
                hi = jnp.where(upper, pltpu.roll(one, 4, 0), two)
                for j, tile in enumerate((lo, hi)):
                    out_ref[first + half * 2 + j, pl.ds(at + pair * 8, 8), :] = tile[:, 0:128]
                    tails[j].append(tile[:, 128:NODES])
            for j in range(2):
                tail = jnp.concatenate([*tails[j], blank], axis=1)
                out_ref[first + half * 2 + j, pl.ds(at + 24, 8), :] = tail


def rotate_mine_kernel(rolled_ref, op_ref, place_ref, out_ref, lines, held, acc):
    contract(rolled_ref, op_ref, lines, held, acc)
    by_target(acc, place_ref[0], out_ref, 0)


def rotate_next_kernel(rolled_ref, op_ref, mine_ref, place_ref, out_ref, lines, held, acc):
    core = place_ref[1]
    out_ref[:, pl.ds(pl.multiple_of(core * 32, 32), 32), :] = mine_ref[...]
    contract(rolled_ref, op_ref, lines, held, acc)
    by_target(acc, place_ref[0], out_ref, pl.multiple_of((1 - core) * 32, 32))


def stokes_kernel(parts_ref, weight_ref, out_ref):
    blob_sq = blob_radius * blob_radius
    total = jnp.zeros((3, 4, 1), F32)
    pole = None
    sums = [jnp.zeros((4, 1), F32) for _ in range(3)]
    for g in range(2 * SIDES):
        here = slice(32 * (g % 2), 32 * (g % 2) + 32)
        whole = parts_ref[g // 2, 0, here, :]
        for b in range(1, BAND):
            whole = whole + parts_ref[g // 2, b, here, :]
        main = [whole[4 * k : 4 * k + 4, :] for k in range(6)]
        tail = whole[24:32, :]
        rest = [
            tail[4 * (k % 2) : 4 * (k % 2) + 4, 32 * (k // 2) : 32 * (k // 2) + 32] for k in range(6)
        ]
        if g == 0:
            pole = [main[k][:, 0:1] for k in range(3)]
        for rows, weights in (
            (main, weight_ref[g : g + 1, 0:128]),
            (rest, weight_ref[g : g + 1, 128:NODES]),
        ):
            d = [pole[k] - rows[k] for k in range(3)]
            f = rows[3:6]
            q = d[0] * d[0] + d[1] * d[1] + d[2] * d[2]
            along = d[0] * f[0] + d[1] * f[1] + d[2] * f[2]
            s = q + blob_sq
            r = lax.rsqrt(s)
            kernel = weights * (r * r * r)
            near = (q + 2.0 * blob_sq) * kernel
            along = along * kernel
            for k in range(3):
                sums[k] = sums[k] + jnp.sum(near * f[k] + along * d[k], axis=1, keepdims=True)
    lane = lax.broadcasted_iota(jnp.int32, (4, 128), 1)
    packed = jnp.where(lane == 0, sums[0], jnp.where(lane == 1, sums[1], sums[2]))
    packed = jnp.concatenate([packed, jnp.zeros((4, 128), F32)], axis=0)
    for b in range(BAND):
        out_ref[b] = packed


def per_device(positions, densities, operator, target_shift, weights):
    vmem = pl.BlockSpec(memory_space=pltpu.VMEM)
    smem = pl.BlockSpec(memory_space=pltpu.SMEM)
    source = jnp.concatenate([positions, densities], axis=1).reshape(144, LON)
    lines, source = pl.pallas_call(
        pack_kernel,
        out_shape=(
            jax.ShapeDtypeStruct((1, SENT_LINES, 128), BF16),
            jax.ShapeDtypeStruct((SOURCE_LINES, 128), BF16),
        ),
        in_specs=[vmem] * 3,
        out_specs=(vmem, vmem),
        scratch_shapes=[pltpu.VMEM((SENT_LINES, 128), F32)],
        compiler_params=pltpu.CompilerParams(vmem_limit_bytes=16 * 2**20),
        name="pack",
    )(operator, source, target_shift)
    other_source = lax.ppermute(source, "y_hi", [(0, 1), (1, 0)])
    mine = lax.all_gather(lines, "z", axis=0, tiled=True)
    mine, other_source = lax.optimization_barrier((mine, other_source))
    other = lax.ppermute(mine, "core", [(0, 1), (1, 0)])
    rolled = pl.pallas_call(
        roll_kernel,
        out_shape=jax.ShapeDtypeStruct((CAPS * 6 * TGT, COLS), BF16),
        in_specs=[vmem] * 2,
        out_specs=vmem,
        scratch_shapes=[pltpu.VMEM((3, SIDES * 144, 128), F32)],
        compiler_params=pltpu.CompilerParams(vmem_limit_bytes=16 * 2**20),
        cost_estimate=pl.CostEstimate(flops=10**9, bytes_accessed=2**22, transcendentals=0),
        name="roll",
    )(source, other_source)
    scratch = [
        pltpu.VMEM((Z * LINES, 128), F32),
        pltpu.VMEM((NODES, COLS), BF16),
        pltpu.VMEM((CAPS * 6 * TGT, NODES), F32),
    ]
    place = jnp.stack([lax.axis_index("y_hi"), lax.axis_index("core")]).astype(jnp.int32)
    parts = pl.pallas_call(
        rotate_mine_kernel,
        out_shape=jax.ShapeDtypeStruct((SIDES * BAND, 32, 128), F32),
        in_specs=[vmem] * 2 + [smem],
        out_specs=vmem,
        scratch_shapes=scratch,
        compiler_params=pltpu.CompilerParams(vmem_limit_bytes=16 * 2**20),
        cost_estimate=pl.CostEstimate(flops=10**9, bytes_accessed=2**22, transcendentals=0),
        name="rotate_mine",
    )(rolled, mine, place)
    parts = pl.pallas_call(
        rotate_next_kernel,
        out_shape=jax.ShapeDtypeStruct((SIDES * BAND, 64, 128), F32),
        in_specs=[vmem] * 3 + [smem],
        out_specs=vmem,
        scratch_shapes=scratch,
        compiler_params=pltpu.CompilerParams(vmem_limit_bytes=16 * 2**20),
        name="rotate_next",
    )(rolled, other, parts, place)
    parts = lax.all_to_all(parts, ("y_hi",) + STRIP, 0, 0, tiled=True)
    weights = weights.reshape(Z, 2 * SIDES, ROWS_HERE).transpose(1, 0, 2)
    weights = weights.reshape(2 * SIDES, NODES)
    found = pl.pallas_call(
        stokes_kernel,
        out_shape=jax.ShapeDtypeStruct((BAND, 8, 128), F32),
        in_specs=[vmem] * 2,
        out_specs=vmem,
        compiler_params=pltpu.CompilerParams(vmem_limit_bytes=16 * 2**20),
        name="stokes",
    )(parts.reshape(SIDES, BAND, 64, 128), weights)
    found = lax.all_to_all(found, STRIP, 0, 0, tiled=True)
    return found[:, 0:4, 0:3].reshape(2, TGT, 3).transpose(0, 2, 1)


def solution(mesh):
    split = Mesh(mesh.devices.reshape(16, 2, 2, 4, 2), CELL + STRIP)
    in_specs = (
        P(CELL, None, STRIP, None),
        P(CELL, None, STRIP, None),
        P(CELL, STRIP, None),
        P(CELL, None),
        P(),
    )
    return jax.shard_map(
        per_device, mesh=split, in_specs=in_specs, out_specs=P(CELL, None, None), check_vma=False
    )
```

```python
import jax
import jax.numpy as jnp
from jax import lax
from jax.experimental import pallas as pl
from jax.experimental.pallas import tpu as pltpu
from jax.sharding import Mesh
from jax.sharding import PartitionSpec as P

F32 = jnp.float32
BF16 = jnp.bfloat16

LAT_HERE = 12
LON = 192
COLS = LAT_HERE * LON
TGT = 16
ROWS_HERE = 10
Z = 16
SIDES = 2
BAND = 8
CAPS = 2 * SIDES
NODES = Z * ROWS_HERE
TILES = COLS // 128
LINES = ROWS_HERE * TILES
SENT_LINES = 184
HIGH_AT = 160
SOURCE_LINES = 240

CELL = ("z", "y_hi", "core")
STRIP = ("x", "y_lo")

blob_radius = 0.5


def pack_kernel(op_ref, source_ref, shift_ref, op_out_ref, source_out_ref, lines):
    for r in range(ROWS_HERE):
        row = op_ref[r].astype(F32)
        high = row[:, 128:LON]
        at = r * TILES
        lines[at : at + LAT_HERE, :] = row[:, 0:128]
        lines[at + LAT_HERE : at + TILES, :] = jnp.concatenate([high[0:6], high[6:12]], axis=1)
    lines[LINES:SENT_LINES, :] = jnp.zeros((SENT_LINES - LINES, 128), F32)
    op_out_ref[0] = lines[...].astype(BF16)
    rows = source_ref[...].astype(F32)
    low = rows[:, 0:128].astype(BF16)
    high = jnp.concatenate([rows[0:72, 128:LON], rows[72:144, 128:LON]], axis=1)
    high = jnp.concatenate([high, jnp.zeros((8, 128), F32)], axis=0).astype(BF16)
    same = lax.broadcasted_iota(jnp.int32, (TGT, TGT), 0) == lax.broadcasted_iota(
        jnp.int32, (TGT, TGT), 1
    )
    columns = []
    for i in range(2):
        shift = jnp.broadcast_to(shift_ref[i : i + 1, :].astype(F32), (TGT, TGT))
        column = jnp.sum(jnp.where(same, shift, 0.0), axis=1, keepdims=True)
        columns.append(jnp.broadcast_to(column, (TGT, 64)))
    columns = jnp.concatenate(columns, axis=1).astype(BF16)
    source_out_ref[0:144, :] = low
    source_out_ref[144:HIGH_AT, :] = columns
    source_out_ref[HIGH_AT:SOURCE_LINES, :] = high


def roll_kernel(src_ref, rolled_ref, tiles):
    for p in range(SIDES):
        high = src_ref[p, HIGH_AT:SOURCE_LINES, :].astype(F32)[0:72, :]
        for i in range(2):
            here = pl.ds(p * 144 + i * 72, 72)
            low = src_ref[p, 0:144, :].astype(F32)[72 * i : 72 * i + 72, :]
            rest = high[:, 64 * i : 64 * i + 64]
            tiles[0, here, :] = low
            tiles[1, here, :] = jnp.concatenate([rest, low[:, 0:64]], axis=1)
            tiles[2, here, :] = jnp.concatenate([low[:, 64:128], rest], axis=1)

    lane = lax.broadcasted_iota(jnp.int32, (TGT, 128), 1)

    def per_capsule(c, carry):
        column = src_ref[c // 2, 144:HIGH_AT, :].astype(F32)
        column = jnp.where(c % 2 == 0, column[:, 0:1], column[:, 64:65])
        shift = jnp.broadcast_to(column.astype(jnp.int32), (TGT, 128))
        take = jnp.bitwise_and(lane + shift, 127)
        goal = jnp.bitwise_and(lane - shift, 127)
        place = goal + shift
        early, late, low = place < 128, place < 256, goal < 64

        def rolled(value):
            return jnp.take_along_axis(value, take, axis=1, mode="promise_in_bounds").astype(BF16)

        for k in range(6):
            base = c * 72 + k * LAT_HERE
            to = pl.ds(pl.multiple_of((c * 6 + k) * TGT, TGT), TGT)

            def row(q, a):
                return jnp.broadcast_to(tiles[q, pl.ds(base + a, 1), :], (TGT, 128))

            for m in range(6):
                t = [row(q, m) for q in range(3)]
                u = [row(q, m + 6) for q in range(3)]
                first = jnp.where(early, t[0], jnp.where(late, t[1], t[2]))
                second = jnp.where(early, u[0], jnp.where(late, u[1], u[2]))
                high = jnp.where(
                    low,
                    jnp.where(early, t[1], t[2]),
                    jnp.where(early, u[2], jnp.where(late, u[0], u[1])),
                )
                rolled_ref[to, m * 128 : m * 128 + 128] = rolled(first)
                rolled_ref[to, (m + 6) * 128 : (m + 6) * 128 + 128] = rolled(second)
                rolled_ref[to, (m + 12) * 128 : (m + 12) * 128 + 128] = rolled(high)
        return carry

    lax.fori_loop(0, CAPS, per_capsule, 0)


def contract(rolled_ref, op_ref, lines, held, acc):
    for z in range(Z):
        lines[z * LINES : (z + 1) * LINES, :] = op_ref[z].astype(F32)[0:LINES, :]
    for n in range(TILES):
        held[:, n * 128 : (n + 1) * 128] = lines[pl.ds(n, NODES, stride=TILES), :].astype(BF16)
    acc[...] = lax.dot_general(
        rolled_ref[...], held[...], (((1,), (1,)), ((), ())), preferred_element_type=F32
    )


def by_target(acc, out_ref, at):
    upper = lax.broadcasted_iota(jnp.int32, (8, NODES), 0) < 4
    blank = jnp.zeros((8, 32), F32)
    for c in range(CAPS):
        first = (c // 2) * BAND + (c % 2) * 4
        for half in range(2):
            tails = [[], []]
            for pair in range(3):
                row = c * 96 + pair * 32 + half * 8
                one = acc[row : row + 8, :]
                two = acc[row + 16 : row + 24, :]
                lo = jnp.where(upper, one, pltpu.roll(two, 4, 0))
                hi = jnp.where(upper, pltpu.roll(one, 4, 0), two)
                for j, tile in enumerate((lo, hi)):
                    out_ref[first + half * 2 + j, pl.ds(at + pair * 8, 8), :] = tile[:, 0:128]
                    tails[j].append(tile[:, 128:NODES])
            for j in range(2):
                tail = jnp.concatenate([*tails[j], blank], axis=1)
                out_ref[first + half * 2 + j, pl.ds(at + 24, 8), :] = tail


def rotate_mine_kernel(rolled_ref, op_ref, out_ref, lines, held, acc):
    contract(rolled_ref, op_ref, lines, held, acc)
    by_target(acc, out_ref, 0)


def rotate_next_kernel(rolled_ref, op_ref, mine_ref, core_ref, out_ref, lines, held, acc):
    core = core_ref[0]
    out_ref[:, pl.ds(pl.multiple_of(core * 32, 32), 32), :] = mine_ref[...]
    contract(rolled_ref, op_ref, lines, held, acc)
    by_target(acc, out_ref, pl.multiple_of((1 - core) * 32, 32))


def stokes_kernel(parts_ref, weight_ref, out_ref):
    blob_sq = blob_radius * blob_radius
    total = jnp.zeros((3, 4, 1), F32)
    pole = None
    sums = [jnp.zeros((4, 1), F32) for _ in range(3)]
    for g in range(2 * SIDES):
        here = slice(32 * (g % 2), 32 * (g % 2) + 32)
        whole = parts_ref[g // 2, 0, here, :]
        for b in range(1, BAND):
            whole = whole + parts_ref[g // 2, b, here, :]
        main = [whole[4 * k : 4 * k + 4, :] for k in range(6)]
        tail = whole[24:32, :]
        rest = [
            tail[4 * (k % 2) : 4 * (k % 2) + 4, 32 * (k // 2) : 32 * (k // 2) + 32] for k in range(6)
        ]
        if g == 0:
            pole = [main[k][:, 0:1] for k in range(3)]
        for rows, weights in (
            (main, weight_ref[g : g + 1, 0:128]),
            (rest, weight_ref[g : g + 1, 128:NODES]),
        ):
            d = [pole[k] - rows[k] for k in range(3)]
            f = rows[3:6]
            q = d[0] * d[0] + d[1] * d[1] + d[2] * d[2]
            along = d[0] * f[0] + d[1] * f[1] + d[2] * f[2]
            s = q + blob_sq
            r = lax.rsqrt(s)
            kernel = weights * (r * r * r)
            near = (q + 2.0 * blob_sq) * kernel
            along = along * kernel
            for k in range(3):
                sums[k] = sums[k] + jnp.sum(near * f[k] + along * d[k], axis=1, keepdims=True)
    lane = lax.broadcasted_iota(jnp.int32, (4, 128), 1)
    packed = jnp.where(lane == 0, sums[0], jnp.where(lane == 1, sums[1], sums[2]))
    packed = jnp.concatenate([packed, jnp.zeros((4, 128), F32)], axis=0)
    for b in range(BAND):
        out_ref[b] = packed


def per_device(positions, densities, operator, target_shift, weights):
    vmem = pl.BlockSpec(memory_space=pltpu.VMEM)
    smem = pl.BlockSpec(memory_space=pltpu.SMEM)
    source = jnp.concatenate([positions, densities], axis=1).reshape(144, LON)
    lines, source = pl.pallas_call(
        pack_kernel,
        out_shape=(
            jax.ShapeDtypeStruct((1, SENT_LINES, 128), BF16),
            jax.ShapeDtypeStruct((SOURCE_LINES, 128), BF16),
        ),
        in_specs=[vmem] * 3,
        out_specs=(vmem, vmem),
        scratch_shapes=[pltpu.VMEM((SENT_LINES, 128), F32)],
        compiler_params=pltpu.CompilerParams(vmem_limit_bytes=16 * 2**20),
        name="pack",
    )(operator, source, target_shift)
    other_source = lax.ppermute(source, "y_hi", [(0, 1), (1, 0)])
    mine = lax.all_gather(lines, "z", axis=0, tiled=True)
    mine, other_source = lax.optimization_barrier((mine, other_source))
    other = lax.ppermute(mine, "core", [(0, 1), (1, 0)])
    first = lax.axis_index("y_hi") == 0
    source = jnp.stack(
        [jnp.where(first, source, other_source), jnp.where(first, other_source, source)]
    )
    rolled = pl.pallas_call(
        roll_kernel,
        out_shape=jax.ShapeDtypeStruct((CAPS * 6 * TGT, COLS), BF16),
        in_specs=[vmem],
        out_specs=vmem,
        scratch_shapes=[pltpu.VMEM((3, SIDES * 144, 128), F32)],
        compiler_params=pltpu.CompilerParams(vmem_limit_bytes=16 * 2**20),
        cost_estimate=pl.CostEstimate(flops=10**9, bytes_accessed=2**22, transcendentals=0),
        name="roll",
    )(source)
    scratch = [
        pltpu.VMEM((Z * LINES, 128), F32),
        pltpu.VMEM((NODES, COLS), BF16),
        pltpu.VMEM((CAPS * 6 * TGT, NODES), F32),
    ]
    core = lax.axis_index("core").astype(jnp.int32)[None]
    parts = pl.pallas_call(
        rotate_mine_kernel,
        out_shape=jax.ShapeDtypeStruct((SIDES * BAND, 32, 128), F32),
        in_specs=[vmem] * 2,
        out_specs=vmem,
        scratch_shapes=scratch,
        compiler_params=pltpu.CompilerParams(vmem_limit_bytes=16 * 2**20),
        cost_estimate=pl.CostEstimate(flops=10**9, bytes_accessed=2**22, transcendentals=0),
        name="rotate_mine",
    )(rolled, mine)
    parts = pl.pallas_call(
        rotate_next_kernel,
        out_shape=jax.ShapeDtypeStruct((SIDES * BAND, 64, 128), F32),
        in_specs=[vmem] * 3 + [smem],
        out_specs=vmem,
        scratch_shapes=scratch,
        compiler_params=pltpu.CompilerParams(vmem_limit_bytes=16 * 2**20),
        name="rotate_next",
    )(rolled, other, parts, core)
    parts = lax.all_to_all(parts, ("y_hi",) + STRIP, 0, 0, tiled=True)
    weights = weights.reshape(Z, 2 * SIDES, ROWS_HERE).transpose(1, 0, 2)
    weights = weights.reshape(2 * SIDES, NODES)
    found = pl.pallas_call(
        stokes_kernel,
        out_shape=jax.ShapeDtypeStruct((BAND, 8, 128), F32),
        in_specs=[vmem] * 2,
        out_specs=vmem,
        compiler_params=pltpu.CompilerParams(vmem_limit_bytes=16 * 2**20),
        name="stokes",
    )(parts.reshape(SIDES, BAND, 64, 128), weights)
    found = lax.all_to_all(found, STRIP, 0, 0, tiled=True)
    return found[:, 0:4, 0:3].reshape(2, TGT, 3).transpose(0, 2, 1)


def solution(mesh):
    split = Mesh(mesh.devices.reshape(16, 2, 2, 4, 2), CELL + STRIP)
    in_specs = (
        P(CELL, None, STRIP, None),
        P(CELL, None, STRIP, None),
        P(CELL, STRIP, None),
        P(CELL, None),
        P(),
    )
    return jax.shard_map(
        per_device, mesh=split, in_specs=in_specs, out_specs=P(CELL, None, None), check_vma=False
    )
```

```python
import jax
import jax.numpy as jnp
from jax import lax
from jax.experimental import pallas as pl
from jax.experimental.pallas import tpu as pltpu
from jax.sharding import Mesh
from jax.sharding import PartitionSpec as P

F32 = jnp.float32
BF16 = jnp.bfloat16

LAT_HERE = 12
LON = 192
COLS = LAT_HERE * LON
TGT = 16
ROWS_HERE = 10
Z = 16
SIDES = 2
BAND = 8
CAPS = 2 * SIDES
NODES = Z * ROWS_HERE
TILES = COLS // 128
LINES = ROWS_HERE * TILES
SENT_LINES = 184
HIGH_AT = 160
SOURCE_LINES = 240

CELL = ("z", "y_hi", "core")
STRIP = ("x", "y_lo")

blob_radius = 0.5


def pack_kernel(op_ref, source_ref, shift_ref, op_out_ref, source_out_ref, lines):
    for r in range(ROWS_HERE):
        row = op_ref[r].astype(F32)
        high = row[:, 128:LON]
        at = r * TILES
        lines[at : at + LAT_HERE, :] = row[:, 0:128]
        lines[at + LAT_HERE : at + TILES, :] = jnp.concatenate([high[0:6], high[6:12]], axis=1)
    lines[LINES:SENT_LINES, :] = jnp.zeros((SENT_LINES - LINES, 128), F32)
    op_out_ref[0] = lines[...].astype(BF16)
    rows = source_ref[...].astype(F32)
    low = rows[:, 0:128].astype(BF16)
    high = jnp.concatenate([rows[0:72, 128:LON], rows[72:144, 128:LON]], axis=1)
    high = jnp.concatenate([high, jnp.zeros((8, 128), F32)], axis=0).astype(BF16)
    same = lax.broadcasted_iota(jnp.int32, (TGT, TGT), 0) == lax.broadcasted_iota(
        jnp.int32, (TGT, TGT), 1
    )
    columns = []
    for i in range(2):
        shift = jnp.broadcast_to(shift_ref[i : i + 1, :].astype(F32), (TGT, TGT))
        column = jnp.sum(jnp.where(same, shift, 0.0), axis=1, keepdims=True)
        columns.append(jnp.broadcast_to(column, (TGT, 64)))
    columns = jnp.concatenate(columns, axis=1).astype(BF16)
    source_out_ref[0:144, :] = low
    source_out_ref[144:HIGH_AT, :] = columns
    source_out_ref[HIGH_AT:SOURCE_LINES, :] = high


def roll_kernel(src_ref, rolled_ref, tiles):
    for p in range(SIDES):
        high = src_ref[p, HIGH_AT:SOURCE_LINES, :].astype(F32)[0:72, :]
        for i in range(2):
            here = pl.ds(p * 144 + i * 72, 72)
            low = src_ref[p, 0:144, :].astype(F32)[72 * i : 72 * i + 72, :]
            rest = high[:, 64 * i : 64 * i + 64]
            tiles[0, here, :] = low
            tiles[1, here, :] = jnp.concatenate([rest, low[:, 0:64]], axis=1)
            tiles[2, here, :] = jnp.concatenate([low[:, 64:128], rest], axis=1)

    lane = lax.broadcasted_iota(jnp.int32, (TGT, 128), 1)

    def per_capsule(c, carry):
        column = src_ref[c // 2, 144:HIGH_AT, :].astype(F32)
        column = jnp.where(c % 2 == 0, column[:, 0:1], column[:, 64:65])
        shift = jnp.broadcast_to(column.astype(jnp.int32), (TGT, 128))
        take = jnp.bitwise_and(lane + shift, 127)
        goal = jnp.bitwise_and(lane - shift, 127)
        place = goal + shift
        early, late, low = place < 128, place < 256, goal < 64

        def rolled(value):
            return jnp.take_along_axis(value, take, axis=1, mode="promise_in_bounds").astype(BF16)

        for k in range(6):
            base = c * 72 + k * LAT_HERE
            to = pl.ds(pl.multiple_of((c * 6 + k) * TGT, TGT), TGT)

            def row(q, a):
                return jnp.broadcast_to(tiles[q, pl.ds(base + a, 1), :], (TGT, 128))

            for m in range(6):
                t = [row(q, m) for q in range(3)]
                u = [row(q, m + 6) for q in range(3)]
                first = jnp.where(early, t[0], jnp.where(late, t[1], t[2]))
                second = jnp.where(early, u[0], jnp.where(late, u[1], u[2]))
                high = jnp.where(
                    low,
                    jnp.where(early, t[1], t[2]),
                    jnp.where(early, u[2], jnp.where(late, u[0], u[1])),
                )
                rolled_ref[to, m * 128 : m * 128 + 128] = rolled(first)
                rolled_ref[to, (m + 6) * 128 : (m + 6) * 128 + 128] = rolled(second)
                rolled_ref[to, (m + 12) * 128 : (m + 12) * 128 + 128] = rolled(high)
        return carry

    lax.fori_loop(0, CAPS, per_capsule, 0)


def contract(rolled_ref, op_ref, lines, held, acc):
    for z in range(Z):
        lines[z * LINES : (z + 1) * LINES, :] = op_ref[z].astype(F32)[0:LINES, :]
    for n in range(TILES):
        held[:, n * 128 : (n + 1) * 128] = lines[pl.ds(n, NODES, stride=TILES), :].astype(BF16)
    acc[...] = lax.dot_general(
        rolled_ref[...], held[...], (((1,), (1,)), ((), ())), preferred_element_type=F32
    )


def by_target(acc, out_ref, at):
    upper = lax.broadcasted_iota(jnp.int32, (8, NODES), 0) < 4
    blank = jnp.zeros((8, 32), F32)
    for c in range(CAPS):
        first = (c // 2) * BAND + (c % 2) * 4
        for half in range(2):
            tails = [[], []]
            for pair in range(3):
                row = c * 96 + pair * 32 + half * 8
                one = acc[row : row + 8, :]
                two = acc[row + 16 : row + 24, :]
                lo = jnp.where(upper, one, pltpu.roll(two, 4, 0))
                hi = jnp.where(upper, pltpu.roll(one, 4, 0), two)
                for j, tile in enumerate((lo, hi)):
                    out_ref[first + half * 2 + j, pl.ds(at + pair * 8, 8), :] = tile[:, 0:128]
                    tails[j].append(tile[:, 128:NODES])
            for j in range(2):
                tail = jnp.concatenate([*tails[j], blank], axis=1)
                out_ref[first + half * 2 + j, pl.ds(at + 24, 8), :] = tail


def rotate_mine_kernel(rolled_ref, op_ref, out_ref, lines, held, acc):
    contract(rolled_ref, op_ref, lines, held, acc)
    by_target(acc, out_ref, 0)


def rotate_next_kernel(
    rolled_ref, op_ref, mine_ref, weight_ref, core_ref, out_ref, weight_out_ref, lines, held, acc
):
    weight_out_ref[...] = weight_ref[...]
    core = core_ref[0]
    out_ref[:, pl.ds(pl.multiple_of(core * 32, 32), 32), :] = mine_ref[...]
    contract(rolled_ref, op_ref, lines, held, acc)
    by_target(acc, out_ref, pl.multiple_of((1 - core) * 32, 32))


def stokes_kernel(parts_ref, weight_ref, out_ref):
    blob_sq = blob_radius * blob_radius
    total = jnp.zeros((3, 4, 1), F32)
    pole = None
    sums = [jnp.zeros((4, 1), F32) for _ in range(3)]
    for g in range(2 * SIDES):
        here = slice(32 * (g % 2), 32 * (g % 2) + 32)
        whole = parts_ref[g // 2, 0, here, :]
        for b in range(1, BAND):
            whole = whole + parts_ref[g // 2, b, here, :]
        main = [whole[4 * k : 4 * k + 4, :] for k in range(6)]
        tail = whole[24:32, :]
        rest = [
            tail[4 * (k % 2) : 4 * (k % 2) + 4, 32 * (k // 2) : 32 * (k // 2) + 32] for k in range(6)
        ]
        if g == 0:
            pole = [main[k][:, 0:1] for k in range(3)]
        for rows, weights in (
            (main, weight_ref[g : g + 1, 0:128]),
            (rest, weight_ref[g : g + 1, 128:NODES]),
        ):
            d = [pole[k] - rows[k] for k in range(3)]
            f = rows[3:6]
            q = d[0] * d[0] + d[1] * d[1] + d[2] * d[2]
            along = d[0] * f[0] + d[1] * f[1] + d[2] * f[2]
            s = q + blob_sq
            r = lax.rsqrt(s)
            kernel = weights * (r * r * r)
            near = (q + 2.0 * blob_sq) * kernel
            along = along * kernel
            for k in range(3):
                sums[k] = sums[k] + jnp.sum(near * f[k] + along * d[k], axis=1, keepdims=True)
    lane = lax.broadcasted_iota(jnp.int32, (4, 128), 1)
    packed = jnp.where(lane == 0, sums[0], jnp.where(lane == 1, sums[1], sums[2]))
    packed = jnp.concatenate([packed, jnp.zeros((4, 128), F32)], axis=0)
    for b in range(BAND):
        out_ref[b] = packed


def per_device(positions, densities, operator, target_shift, weights):
    vmem = pl.BlockSpec(memory_space=pltpu.VMEM)
    smem = pl.BlockSpec(memory_space=pltpu.SMEM)
    source = jnp.concatenate([positions, densities], axis=1).reshape(144, LON)
    lines, source = pl.pallas_call(
        pack_kernel,
        out_shape=(
            jax.ShapeDtypeStruct((1, SENT_LINES, 128), BF16),
            jax.ShapeDtypeStruct((SOURCE_LINES, 128), BF16),
        ),
        in_specs=[vmem] * 3,
        out_specs=(vmem, vmem),
        scratch_shapes=[pltpu.VMEM((SENT_LINES, 128), F32)],
        compiler_params=pltpu.CompilerParams(vmem_limit_bytes=16 * 2**20),
        name="pack",
    )(operator, source, target_shift)
    other_source = lax.ppermute(source, "y_hi", [(0, 1), (1, 0)])
    mine = lax.all_gather(lines, "z", axis=0, tiled=True)
    mine, other_source, weights = lax.optimization_barrier((mine, other_source, weights))
    weights = weights.reshape(Z, 2 * SIDES, ROWS_HERE).transpose(1, 0, 2)
    weights = weights.reshape(2 * SIDES, NODES)
    other = lax.ppermute(mine, "core", [(0, 1), (1, 0)])
    first = lax.axis_index("y_hi") == 0
    source = jnp.stack(
        [jnp.where(first, source, other_source), jnp.where(first, other_source, source)]
    )
    rolled = pl.pallas_call(
        roll_kernel,
        out_shape=jax.ShapeDtypeStruct((CAPS * 6 * TGT, COLS), BF16),
        in_specs=[vmem],
        out_specs=vmem,
        scratch_shapes=[pltpu.VMEM((3, SIDES * 144, 128), F32)],
        compiler_params=pltpu.CompilerParams(vmem_limit_bytes=16 * 2**20),
        cost_estimate=pl.CostEstimate(flops=10**9, bytes_accessed=2**22, transcendentals=0),
        name="roll",
    )(source)
    scratch = [
        pltpu.VMEM((Z * LINES, 128), F32),
        pltpu.VMEM((NODES, COLS), BF16),
        pltpu.VMEM((CAPS * 6 * TGT, NODES), F32),
    ]
    core = lax.axis_index("core").astype(jnp.int32)[None]
    parts = pl.pallas_call(
        rotate_mine_kernel,
        out_shape=jax.ShapeDtypeStruct((SIDES * BAND, 32, 128), F32),
        in_specs=[vmem] * 2,
        out_specs=vmem,
        scratch_shapes=scratch,
        compiler_params=pltpu.CompilerParams(vmem_limit_bytes=16 * 2**20),
        cost_estimate=pl.CostEstimate(flops=10**9, bytes_accessed=2**22, transcendentals=0),
        name="rotate_mine",
    )(rolled, mine)
    parts, weights = pl.pallas_call(
        rotate_next_kernel,
        out_shape=(
            jax.ShapeDtypeStruct((SIDES * BAND, 64, 128), F32),
            jax.ShapeDtypeStruct((2 * SIDES, NODES), F32),
        ),
        in_specs=[vmem] * 4 + [smem],
        out_specs=(vmem, vmem),
        scratch_shapes=scratch,
        compiler_params=pltpu.CompilerParams(vmem_limit_bytes=16 * 2**20),
        name="rotate_next",
    )(rolled, other, parts, weights, core)
    parts = lax.all_to_all(parts, ("y_hi",) + STRIP, 0, 0, tiled=True)
    found = pl.pallas_call(
        stokes_kernel,
        out_shape=jax.ShapeDtypeStruct((BAND, 8, 128), F32),
        in_specs=[vmem] * 2,
        out_specs=vmem,
        compiler_params=pltpu.CompilerParams(vmem_limit_bytes=16 * 2**20),
        name="stokes",
    )(parts.reshape(SIDES, BAND, 64, 128), weights)
    found = lax.all_to_all(found, STRIP, 0, 0, tiled=True)
    return found[:, 0:4, 0:3].reshape(2, TGT, 3).transpose(0, 2, 1)


def solution(mesh):
    split = Mesh(mesh.devices.reshape(16, 2, 2, 4, 2), CELL + STRIP)
    in_specs = (
        P(CELL, None, STRIP, None),
        P(CELL, None, STRIP, None),
        P(CELL, STRIP, None),
        P(CELL, None),
        P(),
    )
    return jax.shard_map(
        per_device, mesh=split, in_specs=in_specs, out_specs=P(CELL, None, None), check_vma=False
    )
```

```python
import jax
import jax.numpy as jnp
from jax import lax
from jax.experimental import pallas as pl
from jax.experimental.pallas import tpu as pltpu
from jax.sharding import Mesh
from jax.sharding import PartitionSpec as P

F32 = jnp.float32
BF16 = jnp.bfloat16

LAT_HERE = 12
LON = 192
COLS = LAT_HERE * LON
TGT = 16
ROWS_HERE = 10
Z = 16
SIDES = 2
BAND = 8
CAPS = 2 * SIDES
NODES = Z * ROWS_HERE
TILES = COLS // 128
LINES = ROWS_HERE * TILES
SENT_LINES = 184
HIGH_AT = 160
SOURCE_LINES = 240

CELL = ("z", "y_hi", "core")
STRIP = ("x", "y_lo")

blob_radius = 0.5


def pack_kernel(op_ref, source_ref, shift_ref, op_out_ref, source_out_ref, lines):
    for r in range(ROWS_HERE):
        row = op_ref[r].astype(F32)
        high = row[:, 128:LON]
        at = r * TILES
        lines[at : at + LAT_HERE, :] = row[:, 0:128]
        lines[at + LAT_HERE : at + TILES, :] = jnp.concatenate([high[0:6], high[6:12]], axis=1)
    lines[LINES:SENT_LINES, :] = jnp.zeros((SENT_LINES - LINES, 128), F32)
    op_out_ref[0] = lines[...].astype(BF16)
    rows = source_ref[...].astype(F32)
    low = rows[:, 0:128].astype(BF16)
    high = jnp.concatenate([rows[0:72, 128:LON], rows[72:144, 128:LON]], axis=1)
    high = jnp.concatenate([high, jnp.zeros((8, 128), F32)], axis=0).astype(BF16)
    same = lax.broadcasted_iota(jnp.int32, (TGT, TGT), 0) == lax.broadcasted_iota(
        jnp.int32, (TGT, TGT), 1
    )
    columns = []
    for i in range(2):
        shift = jnp.broadcast_to(shift_ref[i : i + 1, :].astype(F32), (TGT, TGT))
        column = jnp.sum(jnp.where(same, shift, 0.0), axis=1, keepdims=True)
        columns.append(jnp.broadcast_to(column, (TGT, 64)))
    columns = jnp.concatenate(columns, axis=1).astype(BF16)
    source_out_ref[0:144, :] = low
    source_out_ref[144:HIGH_AT, :] = columns
    source_out_ref[HIGH_AT:SOURCE_LINES, :] = high


def roll_kernel(src_ref, rolled_ref, tiles):
    for p in range(SIDES):
        high = src_ref[p, HIGH_AT:SOURCE_LINES, :].astype(F32)[0:72, :]
        for i in range(2):
            here = pl.ds(p * 144 + i * 72, 72)
            low = src_ref[p, 0:144, :].astype(F32)[72 * i : 72 * i + 72, :]
            rest = high[:, 64 * i : 64 * i + 64]
            tiles[0, here, :] = low
            tiles[1, here, :] = jnp.concatenate([rest, low[:, 0:64]], axis=1)
            tiles[2, here, :] = jnp.concatenate([low[:, 64:128], rest], axis=1)

    lane = lax.broadcasted_iota(jnp.int32, (TGT, 128), 1)

    def per_capsule(c, carry):
        column = src_ref[c // 2, 144:HIGH_AT, :].astype(F32)
        column = jnp.where(c % 2 == 0, column[:, 0:1], column[:, 64:65])
        shift = jnp.broadcast_to(column.astype(jnp.int32), (TGT, 128))
        take = jnp.bitwise_and(lane + shift, 127)
        goal = jnp.bitwise_and(lane - shift, 127)
        place = goal + shift
        early, late, low = place < 128, place < 256, goal < 64

        def rolled(value):
            return jnp.take_along_axis(value, take, axis=1, mode="promise_in_bounds").astype(BF16)

        for k in range(6):
            base = c * 72 + k * LAT_HERE
            to = pl.ds(pl.multiple_of((c * 6 + k) * TGT, TGT), TGT)

            def row(q, a):
                return jnp.broadcast_to(tiles[q, pl.ds(base + a, 1), :], (TGT, 128))

            for m in range(6):
                t = [row(q, m) for q in range(3)]
                u = [row(q, m + 6) for q in range(3)]
                first = jnp.where(early, t[0], jnp.where(late, t[1], t[2]))
                second = jnp.where(early, u[0], jnp.where(late, u[1], u[2]))
                high = jnp.where(
                    low,
                    jnp.where(early, t[1], t[2]),
                    jnp.where(early, u[2], jnp.where(late, u[0], u[1])),
                )
                rolled_ref[to, m * 128 : m * 128 + 128] = rolled(first)
                rolled_ref[to, (m + 6) * 128 : (m + 6) * 128 + 128] = rolled(second)
                rolled_ref[to, (m + 12) * 128 : (m + 12) * 128 + 128] = rolled(high)
        return carry

    lax.fori_loop(0, CAPS, per_capsule, 0)


def contract(rolled_ref, op_ref, lines, held, acc):
    for z in range(Z):
        lines[z * LINES : (z + 1) * LINES, :] = op_ref[z].astype(F32)[0:LINES, :]
    for n in range(TILES):
        held[:, n * 128 : (n + 1) * 128] = lines[pl.ds(n, NODES, stride=TILES), :].astype(BF16)
    acc[...] = lax.dot_general(
        rolled_ref[...], held[...], (((1,), (1,)), ((), ())), preferred_element_type=F32
    )


def by_target(acc, out_ref, at):
    upper = lax.broadcasted_iota(jnp.int32, (8, NODES), 0) < 4
    blank = jnp.zeros((8, 32), F32)
    for c in range(CAPS):
        first = (c // 2) * BAND + (c % 2) * 4
        for half in range(2):
            tails = [[], []]
            for pair in range(3):
                row = c * 96 + pair * 32 + half * 8
                one = acc[row : row + 8, :]
                two = acc[row + 16 : row + 24, :]
                lo = jnp.where(upper, one, pltpu.roll(two, 4, 0))
                hi = jnp.where(upper, pltpu.roll(one, 4, 0), two)
                for j, tile in enumerate((lo, hi)):
                    out_ref[first + half * 2 + j, pl.ds(at + pair * 8, 8), :] = tile[:, 0:128]
                    tails[j].append(tile[:, 128:NODES])
            for j in range(2):
                tail = jnp.concatenate([*tails[j], blank], axis=1)
                out_ref[first + half * 2 + j, pl.ds(at + 24, 8), :] = tail


def rotate_mine_kernel(rolled_ref, op_ref, out_ref, lines, held, acc):
    contract(rolled_ref, op_ref, lines, held, acc)
    by_target(acc, out_ref, 0)


def rotate_next_kernel(
    rolled_ref, op_ref, mine_ref, weight_ref, core_ref, out_ref, weight_out_ref, lines, held, acc
):
    group = 2 * SIDES * ROWS_HERE
    row = weight_ref[...].reshape(1, Z * group)
    for g in range(2 * SIDES):
        parts = [
            row[:, z * group + g * ROWS_HERE : z * group + (g + 1) * ROWS_HERE] for z in range(Z)
        ]
        weight_out_ref[g : g + 1, :] = jnp.concatenate(parts, axis=1)
    core = core_ref[0]
    out_ref[:, pl.ds(pl.multiple_of(core * 32, 32), 32), :] = mine_ref[...]
    contract(rolled_ref, op_ref, lines, held, acc)
    by_target(acc, out_ref, pl.multiple_of((1 - core) * 32, 32))


def stokes_kernel(parts_ref, weight_ref, out_ref):
    blob_sq = blob_radius * blob_radius
    total = jnp.zeros((3, 4, 1), F32)
    pole = None
    sums = [jnp.zeros((4, 1), F32) for _ in range(3)]
    for g in range(2 * SIDES):
        here = slice(32 * (g % 2), 32 * (g % 2) + 32)
        whole = parts_ref[g // 2, 0, here, :]
        for b in range(1, BAND):
            whole = whole + parts_ref[g // 2, b, here, :]
        main = [whole[4 * k : 4 * k + 4, :] for k in range(6)]
        tail = whole[24:32, :]
        rest = [
            tail[4 * (k % 2) : 4 * (k % 2) + 4, 32 * (k // 2) : 32 * (k // 2) + 32] for k in range(6)
        ]
        if g == 0:
            pole = [main[k][:, 0:1] for k in range(3)]
        for rows, weights in (
            (main, weight_ref[g : g + 1, 0:128]),
            (rest, weight_ref[g : g + 1, 128:NODES]),
        ):
            d = [pole[k] - rows[k] for k in range(3)]
            f = rows[3:6]
            q = d[0] * d[0] + d[1] * d[1] + d[2] * d[2]
            along = d[0] * f[0] + d[1] * f[1] + d[2] * f[2]
            s = q + blob_sq
            r = lax.rsqrt(s)
            kernel = weights * (r * r * r)
            near = (q + 2.0 * blob_sq) * kernel
            along = along * kernel
            for k in range(3):
                sums[k] = sums[k] + jnp.sum(near * f[k] + along * d[k], axis=1, keepdims=True)
    lane = lax.broadcasted_iota(jnp.int32, (4, 128), 1)
    packed = jnp.where(lane == 0, sums[0], jnp.where(lane == 1, sums[1], sums[2]))
    packed = jnp.concatenate([packed, jnp.zeros((4, 128), F32)], axis=0)
    for b in range(BAND):
        out_ref[b] = packed


def per_device(positions, densities, operator, target_shift, weights):
    vmem = pl.BlockSpec(memory_space=pltpu.VMEM)
    smem = pl.BlockSpec(memory_space=pltpu.SMEM)
    source = jnp.concatenate([positions, densities], axis=1).reshape(144, LON)
    lines, source = pl.pallas_call(
        pack_kernel,
        out_shape=(
            jax.ShapeDtypeStruct((1, SENT_LINES, 128), BF16),
            jax.ShapeDtypeStruct((SOURCE_LINES, 128), BF16),
        ),
        in_specs=[vmem] * 3,
        out_specs=(vmem, vmem),
        scratch_shapes=[pltpu.VMEM((SENT_LINES, 128), F32)],
        compiler_params=pltpu.CompilerParams(vmem_limit_bytes=16 * 2**20),
        name="pack",
    )(operator, source, target_shift)
    other_source = lax.ppermute(source, "y_hi", [(0, 1), (1, 0)])
    mine = lax.all_gather(lines, "z", axis=0, tiled=True)
    mine, other_source, weights = lax.optimization_barrier((mine, other_source, weights))
    other = lax.ppermute(mine, "core", [(0, 1), (1, 0)])
    first = lax.axis_index("y_hi") == 0
    source = jnp.stack(
        [jnp.where(first, source, other_source), jnp.where(first, other_source, source)]
    )
    rolled = pl.pallas_call(
        roll_kernel,
        out_shape=jax.ShapeDtypeStruct((CAPS * 6 * TGT, COLS), BF16),
        in_specs=[vmem],
        out_specs=vmem,
        scratch_shapes=[pltpu.VMEM((3, SIDES * 144, 128), F32)],
        compiler_params=pltpu.CompilerParams(vmem_limit_bytes=16 * 2**20),
        cost_estimate=pl.CostEstimate(flops=10**9, bytes_accessed=2**22, transcendentals=0),
        name="roll",
    )(source)
    scratch = [
        pltpu.VMEM((Z * LINES, 128), F32),
        pltpu.VMEM((NODES, COLS), BF16),
        pltpu.VMEM((CAPS * 6 * TGT, NODES), F32),
    ]
    core = lax.axis_index("core").astype(jnp.int32)[None]
    parts = pl.pallas_call(
        rotate_mine_kernel,
        out_shape=jax.ShapeDtypeStruct((SIDES * BAND, 32, 128), F32),
        in_specs=[vmem] * 2,
        out_specs=vmem,
        scratch_shapes=scratch,
        compiler_params=pltpu.CompilerParams(vmem_limit_bytes=16 * 2**20),
        cost_estimate=pl.CostEstimate(flops=10**9, bytes_accessed=2**22, transcendentals=0),
        name="rotate_mine",
    )(rolled, mine)
    parts, weights = pl.pallas_call(
        rotate_next_kernel,
        out_shape=(
            jax.ShapeDtypeStruct((SIDES * BAND, 64, 128), F32),
            jax.ShapeDtypeStruct((2 * SIDES, NODES), F32),
        ),
        in_specs=[vmem] * 4 + [smem],
        out_specs=(vmem, vmem),
        scratch_shapes=scratch,
        compiler_params=pltpu.CompilerParams(vmem_limit_bytes=16 * 2**20),
        name="rotate_next",
    )(rolled, other, parts, weights, core)
    parts = lax.all_to_all(parts, ("y_hi",) + STRIP, 0, 0, tiled=True)
    found = pl.pallas_call(
        stokes_kernel,
        out_shape=jax.ShapeDtypeStruct((BAND, 8, 128), F32),
        in_specs=[vmem] * 2,
        out_specs=vmem,
        compiler_params=pltpu.CompilerParams(vmem_limit_bytes=16 * 2**20),
        name="stokes",
    )(parts.reshape(SIDES, BAND, 64, 128), weights)
    found = lax.all_to_all(found, STRIP, 0, 0, tiled=True)
    return found[:, 0:4, 0:3].reshape(2, TGT, 3).transpose(0, 2, 1)


def solution(mesh):
    split = Mesh(mesh.devices.reshape(16, 2, 2, 4, 2), CELL + STRIP)
    in_specs = (
        P(CELL, None, STRIP, None),
        P(CELL, None, STRIP, None),
        P(CELL, STRIP, None),
        P(CELL, None),
        P(),
    )
    return jax.shard_map(
        per_device, mesh=split, in_specs=in_specs, out_specs=P(CELL, None, None), check_vma=False
    )
```

```python
import jax
import jax.numpy as jnp
from jax import lax
from jax.experimental import pallas as pl
from jax.experimental.pallas import tpu as pltpu
from jax.sharding import Mesh
from jax.sharding import PartitionSpec as P

F32 = jnp.float32
BF16 = jnp.bfloat16

LAT_HERE = 12
LON = 192
COLS = LAT_HERE * LON
TGT = 16
ROWS_HERE = 10
Z = 16
SIDES = 2
BAND = 8
CAPS = 2 * SIDES
NODES = Z * ROWS_HERE
TILES = COLS // 128
LINES = ROWS_HERE * TILES
SENT_LINES = 184
HIGH_AT = 160
SOURCE_LINES = 240

CELL = ("z", "y_hi", "core")
STRIP = ("x", "y_lo")

blob_radius = 0.5


def pack_kernel(op_ref, source_ref, shift_ref, op_out_ref, source_out_ref, lines):
    for r in range(ROWS_HERE):
        row = op_ref[r].astype(F32)
        high = row[:, 128:LON]
        at = r * TILES
        lines[at : at + LAT_HERE, :] = row[:, 0:128]
        lines[at + LAT_HERE : at + TILES, :] = jnp.concatenate([high[0:6], high[6:12]], axis=1)
    lines[LINES:SENT_LINES, :] = jnp.zeros((SENT_LINES - LINES, 128), F32)
    op_out_ref[0] = lines[...].astype(BF16)
    rows = source_ref[...].astype(F32)
    low = rows[:, 0:128].astype(BF16)
    high = jnp.concatenate([rows[0:72, 128:LON], rows[72:144, 128:LON]], axis=1)
    high = jnp.concatenate([high, jnp.zeros((8, 128), F32)], axis=0).astype(BF16)
    same = lax.broadcasted_iota(jnp.int32, (TGT, TGT), 0) == lax.broadcasted_iota(
        jnp.int32, (TGT, TGT), 1
    )
    columns = []
    for i in range(2):
        shift = jnp.broadcast_to(shift_ref[i : i + 1, :].astype(F32), (TGT, TGT))
        column = jnp.sum(jnp.where(same, shift, 0.0), axis=1, keepdims=True)
        columns.append(jnp.broadcast_to(column, (TGT, 64)))
    columns = jnp.concatenate(columns, axis=1).astype(BF16)
    source_out_ref[0:144, :] = low
    source_out_ref[144:HIGH_AT, :] = columns
    source_out_ref[HIGH_AT:SOURCE_LINES, :] = high


def roll_kernel(src_ref, rolled_ref, tiles):
    for p in range(SIDES):
        high = src_ref[p, HIGH_AT:SOURCE_LINES, :].astype(F32)[0:72, :]
        for i in range(2):
            here = pl.ds(p * 144 + i * 72, 72)
            low = src_ref[p, 0:144, :].astype(F32)[72 * i : 72 * i + 72, :]
            rest = high[:, 64 * i : 64 * i + 64]
            tiles[0, here, :] = low
            tiles[1, here, :] = jnp.concatenate([rest, low[:, 0:64]], axis=1)
            tiles[2, here, :] = jnp.concatenate([low[:, 64:128], rest], axis=1)

    lane = lax.broadcasted_iota(jnp.int32, (TGT, 128), 1)

    def per_capsule(c, carry):
        column = src_ref[c // 2, 144:HIGH_AT, :].astype(F32)
        column = jnp.where(c % 2 == 0, column[:, 0:1], column[:, 64:65])
        shift = jnp.broadcast_to(column.astype(jnp.int32), (TGT, 128))
        take = jnp.bitwise_and(lane + shift, 127)
        goal = jnp.bitwise_and(lane - shift, 127)
        place = goal + shift
        early, late, low = place < 128, place < 256, goal < 64

        def rolled(value):
            return jnp.take_along_axis(value, take, axis=1, mode="promise_in_bounds").astype(BF16)

        for k in range(6):
            base = c * 72 + k * LAT_HERE
            to = pl.ds(pl.multiple_of((c * 6 + k) * TGT, TGT), TGT)

            def row(q, a):
                return jnp.broadcast_to(tiles[q, pl.ds(base + a, 1), :], (TGT, 128))

            for m in range(6):
                t = [row(q, m) for q in range(3)]
                u = [row(q, m + 6) for q in range(3)]
                first = jnp.where(early, t[0], jnp.where(late, t[1], t[2]))
                second = jnp.where(early, u[0], jnp.where(late, u[1], u[2]))
                high = jnp.where(
                    low,
                    jnp.where(early, t[1], t[2]),
                    jnp.where(early, u[2], jnp.where(late, u[0], u[1])),
                )
                rolled_ref[to, m * 128 : m * 128 + 128] = rolled(first)
                rolled_ref[to, (m + 6) * 128 : (m + 6) * 128 + 128] = rolled(second)
                rolled_ref[to, (m + 12) * 128 : (m + 12) * 128 + 128] = rolled(high)
        return carry

    lax.fori_loop(0, CAPS, per_capsule, 0, unroll=2)


def contract(rolled_ref, op_ref, lines, held, acc):
    for z in range(Z):
        lines[z * LINES : (z + 1) * LINES, :] = op_ref[z].astype(F32)[0:LINES, :]
    for n in range(TILES):
        held[:, n * 128 : (n + 1) * 128] = lines[pl.ds(n, NODES, stride=TILES), :].astype(BF16)
    acc[...] = lax.dot_general(
        rolled_ref[...], held[...], (((1,), (1,)), ((), ())), preferred_element_type=F32
    )


def by_target(acc, out_ref, at):
    upper = lax.broadcasted_iota(jnp.int32, (8, NODES), 0) < 4
    blank = jnp.zeros((8, 32), F32)
    for c in range(CAPS):
        first = (c // 2) * BAND + (c % 2) * 4
        for half in range(2):
            tails = [[], []]
            for pair in range(3):
                row = c * 96 + pair * 32 + half * 8
                one = acc[row : row + 8, :]
                two = acc[row + 16 : row + 24, :]
                lo = jnp.where(upper, one, pltpu.roll(two, 4, 0))
                hi = jnp.where(upper, pltpu.roll(one, 4, 0), two)
                for j, tile in enumerate((lo, hi)):
                    out_ref[first + half * 2 + j, pl.ds(at + pair * 8, 8), :] = tile[:, 0:128]
                    tails[j].append(tile[:, 128:NODES])
            for j in range(2):
                tail = jnp.concatenate([*tails[j], blank], axis=1)
                out_ref[first + half * 2 + j, pl.ds(at + 24, 8), :] = tail


def rotate_mine_kernel(rolled_ref, op_ref, out_ref, lines, held, acc):
    contract(rolled_ref, op_ref, lines, held, acc)
    by_target(acc, out_ref, 0)


def rotate_next_kernel(
    rolled_ref, op_ref, mine_ref, weight_ref, core_ref, out_ref, weight_out_ref, lines, held, acc
):
    group = 2 * SIDES * ROWS_HERE
    row = weight_ref[...].reshape(1, Z * group)
    for g in range(2 * SIDES):
        parts = [
            row[:, z * group + g * ROWS_HERE : z * group + (g + 1) * ROWS_HERE] for z in range(Z)
        ]
        weight_out_ref[g : g + 1, :] = jnp.concatenate(parts, axis=1)
    core = core_ref[0]
    out_ref[:, pl.ds(pl.multiple_of(core * 32, 32), 32), :] = mine_ref[...]
    contract(rolled_ref, op_ref, lines, held, acc)
    by_target(acc, out_ref, pl.multiple_of((1 - core) * 32, 32))


def stokes_kernel(parts_ref, weight_ref, out_ref):
    blob_sq = blob_radius * blob_radius
    total = jnp.zeros((3, 4, 1), F32)
    pole = None
    sums = [jnp.zeros((4, 1), F32) for _ in range(3)]
    for g in range(2 * SIDES):
        here = slice(32 * (g % 2), 32 * (g % 2) + 32)
        whole = parts_ref[g // 2, 0, here, :]
        for b in range(1, BAND):
            whole = whole + parts_ref[g // 2, b, here, :]
        main = [whole[4 * k : 4 * k + 4, :] for k in range(6)]
        tail = whole[24:32, :]
        rest = [
            tail[4 * (k % 2) : 4 * (k % 2) + 4, 32 * (k // 2) : 32 * (k // 2) + 32] for k in range(6)
        ]
        if g == 0:
            pole = [main[k][:, 0:1] for k in range(3)]
        for rows, weights in (
            (main, weight_ref[g : g + 1, 0:128]),
            (rest, weight_ref[g : g + 1, 128:NODES]),
        ):
            d = [pole[k] - rows[k] for k in range(3)]
            f = rows[3:6]
            q = d[0] * d[0] + d[1] * d[1] + d[2] * d[2]
            along = d[0] * f[0] + d[1] * f[1] + d[2] * f[2]
            s = q + blob_sq
            r = lax.rsqrt(s)
            kernel = weights * (r * r * r)
            near = (q + 2.0 * blob_sq) * kernel
            along = along * kernel
            for k in range(3):
                sums[k] = sums[k] + jnp.sum(near * f[k] + along * d[k], axis=1, keepdims=True)
    lane = lax.broadcasted_iota(jnp.int32, (4, 128), 1)
    packed = jnp.where(lane == 0, sums[0], jnp.where(lane == 1, sums[1], sums[2]))
    packed = jnp.concatenate([packed, jnp.zeros((4, 128), F32)], axis=0)
    for b in range(BAND):
        out_ref[b] = packed


def per_device(positions, densities, operator, target_shift, weights):
    vmem = pl.BlockSpec(memory_space=pltpu.VMEM)
    smem = pl.BlockSpec(memory_space=pltpu.SMEM)
    source = jnp.concatenate([positions, densities], axis=1).reshape(144, LON)
    lines, source = pl.pallas_call(
        pack_kernel,
        out_shape=(
            jax.ShapeDtypeStruct((1, SENT_LINES, 128), BF16),
            jax.ShapeDtypeStruct((SOURCE_LINES, 128), BF16),
        ),
        in_specs=[vmem] * 3,
        out_specs=(vmem, vmem),
        scratch_shapes=[pltpu.VMEM((SENT_LINES, 128), F32)],
        compiler_params=pltpu.CompilerParams(vmem_limit_bytes=16 * 2**20),
        name="pack",
    )(operator, source, target_shift)
    other_source = lax.ppermute(source, "y_hi", [(0, 1), (1, 0)])
    mine = lax.all_gather(lines, "z", axis=0, tiled=True)
    mine, other_source, weights = lax.optimization_barrier((mine, other_source, weights))
    other = lax.ppermute(mine, "core", [(0, 1), (1, 0)])
    first = lax.axis_index("y_hi") == 0
    source = jnp.stack(
        [jnp.where(first, source, other_source), jnp.where(first, other_source, source)]
    )
    rolled = pl.pallas_call(
        roll_kernel,
        out_shape=jax.ShapeDtypeStruct((CAPS * 6 * TGT, COLS), BF16),
        in_specs=[vmem],
        out_specs=vmem,
        scratch_shapes=[pltpu.VMEM((3, SIDES * 144, 128), F32)],
        compiler_params=pltpu.CompilerParams(vmem_limit_bytes=16 * 2**20),
        cost_estimate=pl.CostEstimate(flops=10**9, bytes_accessed=2**22, transcendentals=0),
        name="roll",
    )(source)
    scratch = [
        pltpu.VMEM((Z * LINES, 128), F32),
        pltpu.VMEM((NODES, COLS), BF16),
        pltpu.VMEM((CAPS * 6 * TGT, NODES), F32),
    ]
    core = lax.axis_index("core").astype(jnp.int32)[None]
    parts = pl.pallas_call(
        rotate_mine_kernel,
        out_shape=jax.ShapeDtypeStruct((SIDES * BAND, 32, 128), F32),
        in_specs=[vmem] * 2,
        out_specs=vmem,
        scratch_shapes=scratch,
        compiler_params=pltpu.CompilerParams(vmem_limit_bytes=16 * 2**20),
        cost_estimate=pl.CostEstimate(flops=10**9, bytes_accessed=2**22, transcendentals=0),
        name="rotate_mine",
    )(rolled, mine)
    parts, weights = pl.pallas_call(
        rotate_next_kernel,
        out_shape=(
            jax.ShapeDtypeStruct((SIDES * BAND, 64, 128), F32),
            jax.ShapeDtypeStruct((2 * SIDES, NODES), F32),
        ),
        in_specs=[vmem] * 4 + [smem],
        out_specs=(vmem, vmem),
        scratch_shapes=scratch,
        compiler_params=pltpu.CompilerParams(vmem_limit_bytes=16 * 2**20),
        name="rotate_next",
    )(rolled, other, parts, weights, core)
    parts = lax.all_to_all(parts, ("y_hi",) + STRIP, 0, 0, tiled=True)
    found = pl.pallas_call(
        stokes_kernel,
        out_shape=jax.ShapeDtypeStruct((BAND, 8, 128), F32),
        in_specs=[vmem] * 2,
        out_specs=vmem,
        compiler_params=pltpu.CompilerParams(vmem_limit_bytes=16 * 2**20),
        name="stokes",
    )(parts.reshape(SIDES, BAND, 64, 128), weights)
    found = lax.all_to_all(found, STRIP, 0, 0, tiled=True)
    return found[:, 0:4, 0:3].reshape(2, TGT, 3).transpose(0, 2, 1)


def solution(mesh):
    split = Mesh(mesh.devices.reshape(16, 2, 2, 4, 2), CELL + STRIP)
    in_specs = (
        P(CELL, None, STRIP, None),
        P(CELL, None, STRIP, None),
        P(CELL, STRIP, None),
        P(CELL, None),
        P(),
    )
    return jax.shard_map(
        per_device, mesh=split, in_specs=in_specs, out_specs=P(CELL, None, None), check_vma=False
    )
```
